512 devices in a mesh: seq: 128 (over y, z, core), head: 4 (over x).
Axes of the slice: x: 4, y: 8, z: 8, core: 2. Of those that a mesh axis runs over, the one named last changes fastest.
Arguments:
- queries: bfloat16 [32768, 4096], P(('seq', 'head')), may hold values from -1 to 1
- keys: bfloat16 [32768, 1024], P(('seq', 'head')), may hold values from -2.5 to 2.5
- values: bfloat16 [32768, 1024], P(('seq', 'head')), may hold values from -3 to 3
- outputs_saved: bfloat16 [32768, 4096], P(('seq', 'head')), may hold values from -3 to 3
- grad_out: bfloat16 [32768, 4096], P(('seq', 'head')), may hold values from -3 to 3
- lse: float32 [32768, 32], P('seq', 'head'), may hold values from 2.5 to 4
- block_lists: int32 [256, 32, 4], P(None, 'head'), may hold values from 0 to 511, as said below
Outputs:
- grad_queries: bfloat16 [32768, 4096], P(('seq', 'head'))
- grad_keys: bfloat16 [32768, 1024], P(('seq', 'head'))
- grad_values: bfloat16 [32768, 1024], P(('seq', 'head'))
The draws below stay inside these ranges and needn't reach their ends.
Inputs may be any that keep to these rules, and one draw needn't show every extreme that they name: `block_lists`: key block j lies in sequence shard j // 4. No query block lists a key block of its own sequence shard. For the query blocks of one sequence shard and the 8 query heads held by one device along `head`, at most 1 listed block lies in any one other sequence shard; a few shards are listed far more often than the others.
All inputs are finite; a program needn't handle non-finite values.
Results may differ from the reference program's by a relative error of at most 0.011.
Values may be sent and summed in bfloat16 or wider, within the bound.
A program may use at most 128 MiB of HBM per device.

```python
import jax
import jax.numpy as jnp
from jax import lax

QH = 32
KVH = 8
HD = 128
QB = 128
KB = 64
NSEL = 4
TOKENS = 32768
NQB = 256
NKB = 512
NQB_DEV = 2
NKB_DEV = 4
GROUP = 4
N_SEQ = 128
N_HEAD = 4


def draw_block_lists(key, part):
    key = jax.random.fold_in(key, 11)
    neighbour_count = N_SEQ
    heads_dev = QH // N_HEAD
    request_count = NQB_DEV * heads_dev * NSEL
    favoured_count = max(1, neighbour_count // 16)
    key_fav, key_noise, key_shuffle, key_local = jax.random.split(key, 4)
    preferred_blocks = jax.random.permutation(key_fav, neighbour_count - 2)[:favoured_count] + 1
    extra_reward = jnp.zeros((neighbour_count,), jnp.int32).at[preferred_blocks].set(1)
    extra_reward = extra_reward.at[neighbour_count - 1].set(3).at[0].set(2)
    random_jitter = jax.random.randint(key_noise, (neighbour_count, N_HEAD, neighbour_count), 0, 1 << 16)
    owning_devices = jnp.arange(neighbour_count, dtype=jnp.int32)
    logit_scores = (extra_reward[None, None, :] * (1 << 16) + random_jitter) * neighbour_count + owning_devices[None, None, :]
    own_self = owning_devices[:, None, None] == owning_devices[None, None, :]
    logit_scores = jnp.where(own_self, -1, logit_scores)
    ranked = jnp.argsort(-logit_scores, axis=-1, stable=True).astype(jnp.int32)
    shuffle_keys = jax.random.randint(key_shuffle, (neighbour_count, N_HEAD, request_count), 0, 1 << 20)
    shuffle_keys = shuffle_keys * request_count + jnp.arange(request_count, dtype=jnp.int32)[None, None, :]
    shuffled = jnp.argsort(shuffle_keys, axis=-1, stable=True).astype(jnp.int32)
    rank_pos = shuffled % (neighbour_count - 1)
    owner_of = jnp.take_along_axis(ranked, rank_pos, axis=-1)
    local_block = jax.random.randint(key_local, (neighbour_count, N_HEAD, request_count), 0, NKB_DEV)
    local_block = jnp.where(rank_pos == 0, NKB_DEV - 1, jnp.where(rank_pos == 1, 0, local_block))
    chosen = owner_of * NKB_DEV + local_block
    chosen = chosen.reshape(neighbour_count, N_HEAD, NQB_DEV, heads_dev, NSEL).transpose(0, 2, 1, 3, 4)
    return chosen.reshape(NQB, QH, NSEL).astype(jnp.int32)


def steps_of(own_key, extent, pieces, least, top_value):
    def one(position, blocks):
        steps = jax.random.uniform(jax.random.fold_in(jax.random.fold_in(own_key, 6), position), (blocks,), jnp.float32, least / len(pieces), top_value / len(pieces))
        return jnp.repeat(jnp.exp(steps), extent[position] // blocks).reshape((-1,) + (1,) * (len(extent) - position - 1))

    level = one(*pieces[0])
    for cut in pieces[1:]:
        level = level * one(*cut)
    return level


def normal_values(key, dims, spread, reach, cuts=(), kind=jnp.bfloat16):
    entries = spread * jax.random.normal(key, dims, jnp.float32)
    if cuts:
        entries = entries * steps_of(key, dims, cuts, -0.22, 0.18)
    return jnp.clip(entries, -reach, reach).astype(kind)


def setup_inputs(seed: int = 0) -> dict:
    arg_keys = jax.random.split(jax.random.key(seed), 8)
    return {
        "queries": normal_values(arg_keys[0], (TOKENS, QH * HD), 0.4, 1.0, ((0, 512),)),
        "keys": normal_values(arg_keys[1], (TOKENS, KVH * HD), 1.0, 2.5, ((0, 512),)),
        "values": normal_values(arg_keys[2], (TOKENS, KVH * HD), 1.0, 3.0, ((0, 512),)),
        "outputs_saved": normal_values(arg_keys[3], (TOKENS, QH * HD), 1.0, 3.0, ((0, 512),)),
        "grad_out": normal_values(arg_keys[4], (TOKENS, QH * HD), 1.0, 3.0, ((0, 512),)),
        "lse": jnp.clip(2.5 + 1.5 * jax.random.uniform(arg_keys[5], (TOKENS, QH), jnp.float32) ** steps_of(arg_keys[5], (TOKENS, QH), ((0, 128), (1, 4)), -0.2, 0.2), 2.5, 4.0),
        "block_lists": draw_block_lists(jax.random.fold_in(arg_keys[7], 71), 0),
    }


def rounded(tensor):
    return lax.optimization_barrier(tensor.astype(jnp.bfloat16)).astype(jnp.float32)


def remote_terms(q_rows, o_grad, lse_rows, delta_rows, k_rows, v_rows):
    scaling = HD ** -0.5
    q_full = q_rows.astype(jnp.float32)
    o_full = o_grad.astype(jnp.float32)
    k_full = k_rows.astype(jnp.float32)
    v_full = v_rows.astype(jnp.float32)
    logit_scores = jnp.einsum("nkd,nqd->nkq", k_full, q_full) * scaling
    probability = jnp.exp(logit_scores - lse_rows[:, None, :])
    grad_prob = jnp.einsum("nkd,nqd->nkq", v_full, o_full)
    score_gradient = probability * (grad_prob - delta_rows[:, None, :])
    prob_low = rounded(probability)
    score_low = rounded(score_gradient)
    dq_part = (jnp.einsum("nkq,nkd->nqd", score_low, k_full) * scaling).astype(jnp.bfloat16)
    dk_part = (jnp.einsum("nkq,nqd->nkd", score_low, q_full) * scaling).astype(jnp.bfloat16)
    dv_part = jnp.einsum("nkq,nqd->nkd", prob_low, o_full).astype(jnp.bfloat16)
    return dq_part, dk_part, dv_part


def reference(queries, keys, values, outputs_saved, grad_out, lse, block_lists):
    scaling = HD ** -0.5
    ratio = QB // KB
    key_blocks = keys.reshape(NKB, KB, KVH, HD)
    value_blocks = values.reshape(NKB, KB, KVH, HD)
    kv_of_head = jnp.broadcast_to((jnp.arange(QH, dtype=jnp.int32) // GROUP)[:, None], (QH, NSEL)).reshape(-1)
    causal = lax.broadcasted_iota(jnp.int32, (QB, QB), 0) <= lax.broadcasted_iota(jnp.int32, (QB, QB), 1)

    def per_block(totals, block_index):
        grad_k, grad_v = totals
        row_start = block_index * QB
        q_rows = lax.dynamic_slice_in_dim(queries, row_start, QB, 0).reshape(QB, QH, HD)
        do_rows = lax.dynamic_slice_in_dim(grad_out, row_start, QB, 0).reshape(QB, QH, HD)
        o_rows = lax.dynamic_slice_in_dim(outputs_saved, row_start, QB, 0).reshape(QB, QH, HD)
        lse_rows = lax.dynamic_slice_in_dim(lse, row_start, QB, 0)
        delta_rows = jnp.sum(do_rows.astype(jnp.float32) * o_rows.astype(jnp.float32), axis=-1)
        k_rows = lax.dynamic_slice_in_dim(keys, row_start, QB, 0).reshape(QB, KVH, HD).astype(jnp.float32)
        v_rows = lax.dynamic_slice_in_dim(values, row_start, QB, 0).reshape(QB, KVH, HD).astype(jnp.float32)
        q_five = q_rows.reshape(QB, KVH, GROUP, HD).astype(jnp.float32)
        do_five = do_rows.reshape(QB, KVH, GROUP, HD).astype(jnp.float32)
        lse_t = lse_rows.reshape(QB, KVH, GROUP).transpose(1, 2, 0)
        delta_t = delta_rows.reshape(QB, KVH, GROUP).transpose(1, 2, 0)
        logit_scores = jnp.einsum("shd,qhgd->hgsq", k_rows, q_five) * scaling
        probability = jnp.where(causal, jnp.exp(logit_scores - lse_t[:, :, None, :]), jnp.float32(0.0))
        grad_prob = jnp.einsum("shd,qhgd->hgsq", v_rows, do_five)
        score_gradient = probability * (grad_prob - delta_t[:, :, None, :])
        prob_low = rounded(probability)
        score_low = rounded(score_gradient)
        dq_own = (jnp.einsum("hgsq,shd->qhgd", score_low, k_rows) * scaling).reshape(QB, QH, HD)
        dk_own = jnp.einsum("hgsq,qhgd->shd", score_low, q_five) * scaling
        dv_own = jnp.einsum("hgsq,qhgd->shd", prob_low, do_five)
        chosen = block_lists[block_index].reshape(-1)
        k_sel = key_blocks[chosen, :, kv_of_head]
        v_sel = value_blocks[chosen, :, kv_of_head]
        q_sel = jnp.repeat(q_rows.transpose(1, 0, 2), NSEL, axis=0)
        do_sel = jnp.repeat(do_rows.transpose(1, 0, 2), NSEL, axis=0)
        lse_sel = jnp.repeat(lse_rows.T, NSEL, axis=0)
        delta_sel = jnp.repeat(delta_rows.T, NSEL, axis=0)
        dq_part, dk_part, dv_part = remote_terms(q_sel, do_sel, lse_sel, delta_sel, k_sel, v_sel)
        dq_listed = dq_part.astype(jnp.float32).reshape(QH, NSEL, QB, HD).sum(axis=1).transpose(1, 0, 2)
        dq_rows = (dq_own + dq_listed).astype(jnp.bfloat16).reshape(QB, QH * HD)
        block_start = (block_index * ratio).astype(jnp.int32)
        zero = jnp.int32(0)
        old_k = lax.dynamic_slice(grad_k, (block_start, zero, zero, zero), (ratio, KB, KVH, HD))
        old_v = lax.dynamic_slice(grad_v, (block_start, zero, zero, zero), (ratio, KB, KVH, HD))
        grad_k = lax.dynamic_update_slice(grad_k, old_k + dk_own.reshape(ratio, KB, KVH, HD), (block_start, zero, zero, zero))
        grad_v = lax.dynamic_update_slice(grad_v, old_v + dv_own.reshape(ratio, KB, KVH, HD), (block_start, zero, zero, zero))
        grad_k = grad_k.at[chosen, :, kv_of_head].add(dk_part.astype(jnp.float32))
        grad_v = grad_v.at[chosen, :, kv_of_head].add(dv_part.astype(jnp.float32))
        return (grad_k, grad_v), dq_rows

    start_totals = (jnp.zeros((NKB, KB, KVH, HD), jnp.float32), jnp.zeros((NKB, KB, KVH, HD), jnp.float32))
    (grad_k, grad_v), dq_blocks = lax.scan(per_block, start_totals, jnp.arange(NQB, dtype=jnp.int32))
    grad_queries = dq_blocks.reshape(TOKENS, QH * HD)
    grad_keys = grad_k.reshape(TOKENS, KVH * HD).astype(jnp.bfloat16)
    grad_values = grad_v.reshape(TOKENS, KVH * HD).astype(jnp.bfloat16)
    return (grad_queries, grad_keys, grad_values)
```

```python
import functools
import math

import jax
import jax.numpy as jnp
from jax import lax
from jax.experimental import pallas as pl
from jax.experimental.pallas import tpu as pltpu
from jax.sharding import PartitionSpec as P

HD = 128
QB = 128
KB = 64
NSEL = 4
GROUP = 4
MESH = pl.DeviceIdType.MESH
SCALE = HD ** (-0.5)
UNROLL = 4


class Place:
    def __init__(self, R, X):
        self.R, self.X = R, X
        self.x = lax.axis_index("head")
        s = lax.axis_index("seq")
        self.c = s % 2
        self.z = (s // 2) % R
        self.y = s // (2 * R)
        self.qpos = self.qpos_of(self.c)
        self.kpos = self.qpos_of(1 - self.c)
        self.me = self.c * X + self.x

    def qpos_of(self, c):
        return c * self.y + (1 - c) * self.z

    def dev(self, y, z, c, x):
        return ((y * self.R + z) * 2 + c, x)

    def peer(self, j):
        c = (self.c + j % 2) % 2
        x = (self.x + j // 2) % self.X
        return c, x

    def peer_dev(self, j):
        c, x = self.peer(j)
        return self.dev(self.y, self.z, c, x)

    def src(self, j):
        c, x = self.peer(j)
        return c * self.X + x

    def q_next(self, d):
        d = d % self.R
        y = (self.y + self.c * d) % self.R
        z = (self.z + (1 - self.c) * d) % self.R
        return self.dev(y, z, self.c, self.x)

    def k_next(self, d):
        d = d % self.R
        y = (self.y + (1 - self.c) * d) % self.R
        z = (self.z + self.c * d) % self.R
        return self.dev(y, z, self.c, self.x)

    def barrier(self):
        sem = pltpu.get_barrier_semaphore()
        others = [self.peer_dev(j) for j in range(1, 2 * self.X)]
        others += [self.q_next(1), self.q_next(-1), self.k_next(1), self.k_next(-1)]
        for other in others:
            pl.semaphore_signal(sem, inc=1, device_id=other, device_id_type=MESH)
        pl.semaphore_wait(sem, len(others))


def gather_kernel(
    R, X, q, do, k, v, dl, ls, QD, KV, ST, xs, xr, ls_s, ls_r, loc, qs, qr, ks, kr, ss, sr
):
    p = Place(R, X)
    N = 2 * X
    K = R // 2
    p.barrier()

    def remote(src, dst, s_sem, r_sem, to):
        return pltpu.make_async_remote_copy(
            src_ref=src, dst_ref=dst, send_sem=s_sem, recv_sem=r_sem, device_id=to, device_id_type=MESH
        )

    def pieces(j):
        cj, xj = p.peer(j)
        kvh = 2 * xj + cj
        qcol = pl.ds(pl.multiple_of(kvh * (GROUP * HD), GROUP * HD), GROUP * HD)
        kcol = pl.ds(pl.multiple_of(kvh * HD, HD), HD)
        qp, kp = p.qpos_of(cj), p.qpos_of(1 - cj)
        return (
            (q.at[:, qcol], QD.at[qp, p.me, 0]),
            (do.at[:, qcol], QD.at[qp, p.me, 1]),
            (k.at[:, kcol], KV.at[kp, p.me, 0]),
            (v.at[:, kcol], KV.at[kp, p.me, 1]),
            (dl.at[kvh], ST.at[qp, p.me]),
        )

    def x_send(j, i):
        src, dst = pieces(j)[i]
        return remote(src, dst, xs.at[i, j], xr.at[i, p.me], p.peer_dev(j))

    def x_wait(j, i):
        n = p.src(j)
        dst = (QD.at[p.qpos, n, 0], QD.at[p.qpos, n, 1], KV.at[p.kpos, n, 0], KV.at[p.kpos, n, 1], ST.at[p.qpos, n])[i]
        remote(dst, dst, xs.at[i, j], xr.at[i, n], p.peer_dev(j)).wait_recv()

    other = p.dev(p.y, p.z, 1 - p.c, p.x)
    own_copies = [
        pltpu.make_async_copy(src, dst, loc.at[i]) for i, (src, dst) in enumerate(pieces(0))
    ]
    own_copies.append(pltpu.make_async_copy(ls.at[p.c], ST.at[p.qpos, N + p.c], loc.at[5]))
    for copy in own_copies:
        copy.start()
    for j in range(1, N):
        for i in range(5):
            x_send(j, i).start()
    oc = 1 - p.c
    ls_copy = remote(ls.at[oc], ST.at[p.qpos_of(oc), N + p.c], ls_s, ls_r, other)
    ls_copy.start()
    ls_back = remote(
        ST.at[p.qpos, N + oc], ST.at[p.qpos, N + oc], ls_s, ls_r, other
    )

    def q_copy(d, step, j):
        shift = R - (step - 1) if d == 0 else step - 1
        b = (p.qpos + shift) % R
        n = p.src(j)
        return remote(QD.at[b, n], QD.at[b, n], qs.at[d, step - 1, j], qr.at[d, step - 1, j], p.q_next(1 - 2 * d))

    def q_wait(d, step, j):
        shift = R - step if d == 0 else step
        b = (p.qpos + shift) % R
        n = p.src(j)
        remote(QD.at[b, n], QD.at[b, n], qs.at[d, step - 1, j], qr.at[d, step - 1, j], p.q_next(1 - 2 * d)).wait_recv()

    def k_copy(d, step, h):
        shift = R - (step - 1) if d == 0 else step - 1
        b = (p.kpos + shift) % R
        part = KV.at[b, pl.ds(h * X, X)]
        return remote(part, part, ks.at[d, step - 1, h], kr.at[d, step - 1, h], p.k_next(1 - 2 * d))

    def k_wait(d, step, h):
        shift = R - step if d == 0 else step
        b = (p.kpos + shift) % R
        part = KV.at[b, pl.ds(h * X, X)]
        remote(part, part, ks.at[d, step - 1, h], kr.at[d, step - 1, h], p.k_next(1 - 2 * d)).wait_recv()

    def s_copy(d, step):
        shift = R - (step - 1) if d == 0 else step - 1
        b = (p.qpos + shift) % R
        return remote(ST.at[b], ST.at[b], ss.at[d, step - 1], sr.at[d, step - 1], p.q_next(1 - 2 * d))

    def s_wait(d, step):
        shift = R - step if d == 0 else step
        b = (p.qpos + shift) % R
        remote(ST.at[b], ST.at[b], ss.at[d, step - 1], sr.at[d, step - 1], p.q_next(1 - 2 * d)).wait_recv()

    own_copies[0].wait()
    own_copies[1].wait()
    q_copy(0, 1, 0).start()
    q_copy(1, 1, 0).start()

    @pl.loop(1, N)
    def _(j):
        x_wait(j, 0)
        x_wait(j, 1)
        q_copy(0, 1, j).start()
        q_copy(1, 1, j).start()

    for copy in own_copies[2:]:
        copy.wait()

    @pl.loop(1, N)
    def _(j):
        for i in (2, 3, 4):
            x_wait(j, i)

    ls_back.wait_recv()
    for h in range(2):
        k_copy(0, 1, h).start()
        k_copy(1, 1, h).start()
    s_copy(0, 1).start()
    s_copy(1, 1).start()

    for step in range(2, K + 1):
        last = step == K

        def both(j, right=True, left=True, step=step):
            q_wait(0, step - 1, j)
            if right:
                q_copy(0, step, j).start()
            q_wait(1, step - 1, j)
            if left:
                q_copy(1, step, j).start()

        if not last:
            pl.loop(0, N)(both)
        else:
            pl.loop(0, X)(functools.partial(both, left=False))
            pl.loop(X, N)(functools.partial(both, right=False))
        for h in range(2):
            k_wait(0, step - 1, h)
            if not last or h == 0:
                k_copy(0, step, h).start()
            k_wait(1, step - 1, h)
            if not last or h == 1:
                k_copy(1, step, h).start()
        s_wait(0, step - 1)
        s_copy(0, step).start()
        s_wait(1, step - 1)
        if not last:
            s_copy(1, step).start()

    @pl.loop(0, X)
    def _(j):
        q_wait(0, K, j)
        q_wait(1, K, j + X)

    k_wait(0, K, 0)
    k_wait(1, K, 1)
    s_wait(0, K)

    @pl.loop(1, N)
    def _(j):
        for i in range(5):
            x_send(j, i).wait_send()

    ls_copy.wait_send()
    for step in range(1, K + 1):
        if step < K:

            @pl.loop(0, N)
            def _(j, step=step):
                q_copy(0, step, j).wait_send()
                q_copy(1, step, j).wait_send()

        else:

            @pl.loop(0, X)
            def _(j):
                q_copy(0, K, j).wait_send()
                q_copy(1, K, j + X).wait_send()

        for h in range(2):
            if step < K or h == 0:
                k_copy(0, step, h).wait_send()
            if step < K or h == 1:
                k_copy(1, step, h).wait_send()
        s_copy(0, step).wait_send()
        if step < K:
            s_copy(1, step).wait_send()


def gather(R, X, q, do, k, v, dl, ls):
    N, K = 2 * X, R // 2
    rows = q.shape[0]
    anyspace = pl.BlockSpec(memory_space=pl.ANY)
    dma = pltpu.SemaphoreType.DMA
    return pl.pallas_call(
        functools.partial(gather_kernel, R, X),
        out_shape=(
            jax.ShapeDtypeStruct((R, N, 2, rows, GROUP * HD), jnp.bfloat16),
            jax.ShapeDtypeStruct((R, N, 2, rows, HD), jnp.bfloat16),
            jax.ShapeDtypeStruct((R, N + 2, 8, 128), jnp.float32),
        ),
        in_specs=[anyspace] * 6,
        out_specs=(anyspace,) * 3,
        scratch_shapes=[
            dma((5, N)),
            dma((5, N)),
            dma,
            dma,
            dma((6,)),
            dma((2, K, N)),
            dma((2, K, N)),
            dma((2, K, 2)),
            dma((2, K, 2)),
            dma((2, K)),
            dma((2, K)),
        ],
        compiler_params=pltpu.CompilerParams(collective_id=1, has_side_effects=True),
        name="gather_rings",
    )(q, do, k, v, dl, ls)


def dot(a, b, ca, cb):
    return lax.dot_general(a, b, (((ca,), (cb,)), ((), ())), preferred_element_type=jnp.float32)


def pair_kernel(X, pairs, info, QD, KV, ST, dq_out, kv_out, oq, okv, dq, dkv):
    R, N = QD.shape[0], QD.shape[1]
    c, qpos, kpos, count = info[0], info[1], info[2], info[3]
    half = QB // 2

    @pl.loop(0, R * N)
    def _(i):
        dq[i // N, i % N] = jnp.zeros(dq.shape[2:], jnp.float32)
        dkv[i // N, i % N] = jnp.zeros(dkv.shape[2:], jnp.float32)

    def heads(p, s0, g):
        return pl.ds(s0, 2), pl.ds(pl.multiple_of(g * HD, HD), HD)

    def load_query(p, s0, g):
        rows, cols = heads(p, s0, g)
        qv = QD[p, rows, 0, :, cols].reshape(QB, HD)
        dov = QD[p, rows, 1, :, cols].reshape(QB, HD)
        b = (s0 // 2) % 2
        shard = s0 // X
        lse = ST[p, N + shard, pl.ds(b * GROUP + g, 1), :]
        delta = ST[p, s0, pl.ds(g, 1), :] + ST[p, s0 + 1, pl.ds(g, 1), :]
        return qv, dov, lse, delta

    def grads(qv, dov, lse, delta, kv, vv, mask=None):
        prob = jnp.exp(dot(kv, qv, 1, 1) * SCALE - lse)
        if mask is not None:
            prob = jnp.where(mask, prob, 0.0)
        ds = (prob * (dot(vv, dov, 1, 1) - delta)).astype(jnp.bfloat16)
        pb = prob.astype(jnp.bfloat16)
        return dot(ds, kv, 0, 0), dot(ds, qv, 1, 0), dot(pb, dov, 1, 0)

    causal = lax.broadcasted_iota(jnp.int32, (QB, QB), 0) <= lax.broadcasted_iota(jnp.int32, (QB, QB), 1)

    @pl.loop(0, N // 2)
    def _(blk):
        s0 = blk * 2
        kv = KV[kpos, pl.ds(s0, 2), 0].reshape(QB, HD)
        vv = KV[kpos, pl.ds(s0, 2), 1].reshape(QB, HD)
        results = []
        for g in range(GROUP):
            results.append(grads(*load_query(qpos, s0, g), kv, vv, causal))
        for g in range(GROUP):
            dq[qpos, pl.ds(s0, 2), :, g * HD : (g + 1) * HD] = results[g][0].reshape(2, half, HD)
        dkv[kpos, pl.ds(s0, 2), 0] = sum(r[1] for r in results).reshape(2, half, HD)
        dkv[kpos, pl.ds(s0, 2), 1] = sum(r[2] for r in results).reshape(2, half, HD)

    @pl.loop(0, (count + UNROLL - 1) // UNROLL)
    def _(t):
        results = []
        for u in range(UNROLL):
            i = t * UNROLL + u
            code = pairs[i]
            unit, key = code // (R * N), code % (R * N)
            g = unit % GROUP
            blk = unit // GROUP
            p, s0 = blk // (N // 2), (blk % (N // 2)) * 2
            kp, kn = key // N, key % N
            qv, dov, lse, delta = load_query(p, s0, g)
            lse = lse + jnp.where(i < count, 0.0, 1e30)
            out = grads(qv, dov, lse, delta, KV[kp, kn, 0], KV[kp, kn, 1])
            results.append((p, s0, g, kp, kn, out))
        for p, s0, g, kp, kn, out in results:
            rows, cols = heads(p, s0, g)
            dq[p, rows, :, cols] += out[0].reshape(2, half, HD)
            dkv[kp, kn, 0] += out[1]
            dkv[kp, kn, 1] += out[2]

    @pl.loop(0, R * N)
    def _(i):
        dq_out[i // N, i % N] = (dq[i // N, i % N] * SCALE).astype(jnp.bfloat16)
        kv_out[i // N, i % N, 0] = (dkv[i // N, i % N, 0] * SCALE).astype(jnp.bfloat16)
        kv_out[i // N, i % N, 1] = dkv[i // N, i % N, 1].astype(jnp.bfloat16)

    @pl.loop(0, N)
    def _(n):
        oq[n] = dq[qpos, n] * SCALE
        okv[n, 0] = dkv[kpos, n, 0] * SCALE
        okv[n, 1] = dkv[kpos, n, 1]


def pair_grads(X, pairs, info, QD, KV, ST):
    vmem = pl.BlockSpec(memory_space=pltpu.VMEM)
    smem = pl.BlockSpec(memory_space=pltpu.SMEM)
    q_shape = QD.shape[:2] + QD.shape[3:]
    return pl.pallas_call(
        functools.partial(pair_kernel, X),
        out_shape=(
            jax.ShapeDtypeStruct(q_shape, jnp.bfloat16),
            jax.ShapeDtypeStruct(KV.shape, jnp.bfloat16),
            jax.ShapeDtypeStruct(q_shape[1:], jnp.float32),
            jax.ShapeDtypeStruct(KV.shape[1:], jnp.float32),
        ),
        in_specs=[smem, smem, vmem, vmem, vmem],
        out_specs=(vmem,) * 4,
        scratch_shapes=[pltpu.VMEM(q_shape, jnp.float32), pltpu.VMEM(KV.shape, jnp.float32)],
        compiler_params=pltpu.CompilerParams(vmem_limit_bytes=50 << 20),
        name="pair_grads",
    )(pairs, info, QD, KV, ST)


def reduce_kernel(
    R, X, dq, dkv, oq, okv, gq, gk, gv, rq, rk, bq, bk, xs, xr, loc, qs, qr, ks, kr
):
    p = Place(R, X)
    N = 2 * X
    K = R // 2
    p.barrier()

    def remote(src, dst, s_sem, r_sem, to):
        return pltpu.make_async_remote_copy(
            src_ref=src, dst_ref=dst, send_sem=s_sem, recv_sem=r_sem, device_id=to, device_id_type=MESH
        )

    def owner(pos, d, step):
        far = K + 1 - step
        return (pos + (far if d == 0 else R - far)) % R

    def q_send(src, d, step, j):
        return remote(src, rq.at[d, step - 1, j], qs.at[d, step - 1, j], qr.at[d, step - 1, j], p.q_next(1 - 2 * d))

    def q_wait(d, step, j):
        buf = rq.at[d, step - 1, j]
        q_send(buf, d, step, j).wait_recv()

    def k_send(src, d, step, h):
        return remote(src, rk.at[d, step - 1, h], ks.at[d, step - 1, h], kr.at[d, step - 1, h], p.k_next(1 - 2 * d))

    def k_wait(d, step, h):
        buf = rk.at[d, step - 1, h]
        k_send(buf, d, step, h).wait_recv()

    def q_add(d, step, j):
        q_wait(d, step - 1, j)
        buf = rq.at[d, step - 2, j]
        mine = dq[owner(p.qpos, d, step), p.src(j)]
        buf[...] = (buf[...].astype(jnp.float32) + mine.astype(jnp.float32)).astype(jnp.bfloat16)
        q_send(buf, d, step, j).start()

    def q_plain(d, step, j):
        q_send(dq.at[owner(p.qpos, d, step), p.src(j)], d, step, j).start()

    def k_add(d, step, h):
        k_wait(d, step - 1, h)
        buf = rk.at[d, step - 2, h]
        mine = dkv[owner(p.kpos, d, step), pl.ds(h * X, X)]
        buf[...] = (buf[...].astype(jnp.float32) + mine.astype(jnp.float32)).astype(jnp.bfloat16)
        k_send(buf, d, step, h).start()

    def k_plain(d, step, h):
        k_send(dkv.at[owner(p.kpos, d, step), pl.ds(h * X, X)], d, step, h).start()

    @pl.loop(0, X)
    def _(j):
        q_plain(0, 1, j)
        q_plain(1, 1, j + X)

    k_plain(0, 1, 0)
    k_plain(1, 1, 1)

    @pl.loop(0, X)
    def _(j):
        q_plain(0, 2, j + X)
        q_plain(1, 2, j)

    k_plain(0, 2, 1)
    k_plain(1, 2, 0)

    @pl.loop(0, X)
    def _(j):
        q_add(0, 2, j)
        q_add(1, 2, j + X)

    k_add(0, 2, 0)
    k_add(1, 2, 1)

    for step in range(3, K + 1):

        @pl.loop(0, N)
        def _(j, step=step):
            q_add(0, step, (j + X) % N)
            q_add(1, step, j)

        for h in range(2):
            k_add(0, step, 1 - h)
            k_add(1, step, h)

    qcol = pl.ds(pl.multiple_of((2 * p.x + p.c) * (GROUP * HD), GROUP * HD), GROUP * HD)
    kcol = pl.ds(pl.multiple_of((2 * p.x + p.c) * HD, HD), HD)

    def x_copies(j):
        n = p.src(j)
        return (
            (bq.at[n], gq.at[:, qcol]),
            (bk.at[n, 0], gk.at[:, kcol]),
            (bk.at[n, 1], gv.at[:, kcol]),
        )

    def x_send(j, i):
        src, dst = x_copies(j)[i]
        return remote(src, dst, xs.at[i, j], xr.at[i, p.me], p.peer_dev(j))

    def q_total(j):
        q_wait(0, K, j)
        q_wait(1, K, j)
        n = p.src(j)
        bq[n] = (oq[n] + rq[0, K - 1, j].astype(jnp.float32) + rq[1, K - 1, j].astype(jnp.float32)).astype(jnp.bfloat16)

    @pl.loop(1, N)
    def _(j):
        q_total(j)
        x_send(j, 0).start()

    q_total(0)
    own = [pltpu.make_async_copy(src, dst, loc.at[i]) for i, (src, dst) in enumerate(x_copies(0))]
    own[0].start()
    for h in range(2):
        k_wait(0, K, h)
        k_wait(1, K, h)
        part = pl.ds(h * X, X)
        bk[part] = (
            okv[part] + rk[0, K - 1, h].astype(jnp.float32) + rk[1, K - 1, h].astype(jnp.float32)
        ).astype(jnp.bfloat16)

    @pl.loop(1, N)
    def _(j):
        x_send(j, 1).start()
        x_send(j, 2).start()

    own[1].start()
    own[2].start()

    def x_wait(j, i):
        cj, xj = p.peer(j)
        n = p.src(j)
        qc = pl.ds(pl.multiple_of((2 * xj + cj) * (GROUP * HD), GROUP * HD), GROUP * HD)
        kc = pl.ds(pl.multiple_of((2 * xj + cj) * HD, HD), HD)
        dst = (gq.at[:, qc], gk.at[:, kc], gv.at[:, kc])[i]
        src = (bq.at[n], bk.at[n, 0], bk.at[n, 1])[i]
        remote(src, dst, xs.at[i, j], xr.at[i, n], p.peer_dev(j)).wait_recv()

    @pl.loop(1, N)
    def _(j):
        for i in range(3):
            x_wait(j, i)
            x_send(j, i).wait_send()

    for copy in own:
        copy.wait()

    @pl.loop(0, X)
    def _(j):
        q_plain_wait(q_send, rq, 1, j, X)

    for step in range(2, K + 1):

        @pl.loop(0, N)
        def _(j, step=step):
            for d in range(2):
                q_send(rq.at[d, step - 1, j], d, step, j).wait_send()

    k_send(rk.at[0, 0, 0], 0, 1, 0).wait_send()
    k_send(rk.at[1, 0, 1], 1, 1, 1).wait_send()
    for step in range(2, K + 1):
        for h in range(2):
            for d in range(2):
                k_send(rk.at[d, step - 1, h], d, step, h).wait_send()


def q_plain_wait(q_send, rq, step, j, X):
    q_send(rq.at[0, step - 1, j], 0, step, j).wait_send()
    q_send(rq.at[1, step - 1, j + X], 1, step, j + X).wait_send()


def reduce(R, X, dq, dkv, oq, okv):
    N, K = 2 * X, R // 2
    rows = dq.shape[2]
    anyspace = pl.BlockSpec(memory_space=pl.ANY)
    vmem = pl.BlockSpec(memory_space=pltpu.VMEM)
    dma = pltpu.SemaphoreType.DMA
    return pl.pallas_call(
        functools.partial(reduce_kernel, R, X),
        out_shape=(
            jax.ShapeDtypeStruct((rows, N * GROUP * HD), jnp.bfloat16),
            jax.ShapeDtypeStruct((rows, N * HD), jnp.bfloat16),
            jax.ShapeDtypeStruct((rows, N * HD), jnp.bfloat16),
        ),
        in_specs=[vmem] * 4,
        out_specs=(anyspace,) * 3,
        scratch_shapes=[
            pltpu.VMEM((2, K, N) + dq.shape[2:], jnp.bfloat16),
            pltpu.VMEM((2, K, 2, X) + dkv.shape[2:], jnp.bfloat16),
            pltpu.VMEM(oq.shape, jnp.bfloat16),
            pltpu.VMEM(okv.shape, jnp.bfloat16),
            dma((3, N)),
            dma((3, N)),
            dma((3,)),
            dma((2, K, N)),
            dma((2, K, N)),
            dma((2, K, 2)),
            dma((2, K, 2)),
        ],
        compiler_params=pltpu.CompilerParams(
            collective_id=2, has_side_effects=True, vmem_limit_bytes=40 << 20
        ),
        name="reduce_rings",
    )(dq, dkv, oq, okv)


def list_pairs(R, X, block_lists):
    s = lax.axis_index("seq")
    c, z, y = s % 2, (s // 2) % R, s // (2 * R)
    lists = block_lists.reshape(R, R, 2, 2, 2, GROUP * NSEL)
    lists = lax.dynamic_index_in_dim(lists, c, 4, keepdims=False)
    along_z = lax.dynamic_index_in_dim(lists, y, 0, keepdims=False)
    along_y = lax.dynamic_index_in_dim(lists, z, 1, keepdims=False)
    mine = jnp.where(c == 0, along_z, along_y).reshape(-1)
    per_shard = X
    shard, local = mine // per_shard, mine % per_shard
    ky, kz, kc = shard // (2 * R), (shard // 2) % R, shard % 2
    here = jnp.where(c == 0, kz == z, ky == y)
    kp = jnp.where(c == 0, ky, kz)
    n = mine.shape[0]
    unit = jnp.arange(n, dtype=jnp.int32) // NSEL
    code = unit * (R * 2 * X) + kp * (2 * X) + kc * X + local
    ids = jnp.arange(n, dtype=jnp.int32)
    rank = jnp.sum((here[None, :] & (ids[None, :] < ids[:, None])).astype(jnp.int32), axis=1)
    hit = (rank[None, :] == ids[:, None]) & here[None, :]
    packed = jnp.sum(jnp.where(hit, code[None, :], 0), axis=1)
    count = jnp.sum(here.astype(jnp.int32))
    qpos, kpos = c * y + (1 - c) * z, c * z + (1 - c) * y
    return packed, jnp.stack([c, qpos, kpos, count]).astype(jnp.int32)


def body(R, X, queries, keys, values, outputs_saved, grad_out, lse, block_lists):
    rows = queries.shape[0]
    x = lax.axis_index("head")
    products = grad_out.astype(jnp.float32) * outputs_saved.astype(jnp.float32)
    delta = jnp.sum(products.reshape(rows, -1, HD), axis=-1).T
    delta = delta.reshape(2 * X, GROUP, rows)
    none = jnp.zeros_like(delta)
    odd = x % 2 == 1
    delta = jnp.concatenate([jnp.where(odd, none, delta), jnp.where(odd, delta, none)], axis=-1)
    delta = jnp.pad(delta, ((0, 0), (0, 8 - GROUP), (0, 0)))
    stats = lse.reshape(2, QB, 2, GROUP).transpose(2, 0, 3, 1).reshape(2, 2 * GROUP, QB)
    QD, KV, ST = gather(R, X, queries, grad_out, keys, values, delta, stats)
    pairs, info = list_pairs(R, X, block_lists)
    dq, dkv, oq, okv = pair_grads(X, pairs, info, QD, KV, ST)
    return reduce(R, X, dq, dkv, oq, okv)


def solution(mesh):
    R = math.isqrt(mesh.shape["seq"] // 2)
    X = mesh.shape["head"]
    in_specs = (
        P(("seq", "head"), None),
        P(("seq", "head"), None),
        P(("seq", "head"), None),
        P(("seq", "head"), None),
        P(("seq", "head"), None),
        P("seq", "head"),
        P(None, "head", None),
    )
    out_specs = (P(("seq", "head"), None), P(("seq", "head"), None), P(("seq", "head"), None))
    return jax.shard_map(
        functools.partial(body, R, X), mesh=mesh, in_specs=in_specs, out_specs=out_specs, check_vma=False
    )
```

```python
import functools
import math

import jax
import jax.numpy as jnp
from jax import lax
from jax.experimental import pallas as pl
from jax.experimental.pallas import tpu as pltpu
from jax.sharding import PartitionSpec as P

HD = 128
QB = 128
KB = 64
NSEL = 4
GROUP = 4
WIDE = GROUP * HD
MESH = pl.DeviceIdType.MESH
SCALE = HD ** (-0.5)
UNROLL = 4


class Place:
    def __init__(self, R, X):
        self.R, self.X = R, X
        self.x = lax.axis_index("head")
        s = lax.axis_index("seq")
        self.c = s % 2
        self.z = (s // 2) % R
        self.y = s // (2 * R)

    def dev(self, dx=0, dy=0, dz=0):
        return self.at((self.x + dx) % self.X, (self.y + dy) % self.R, (self.z + dz) % self.R)

    def at(self, x, y, z):
        return ((y * self.R + z) * 2 + self.c, x)

    def sibling(self):
        return ((self.y * self.R + self.z) * 2 + 1 - self.c, self.x)

    def far(self, t):
        return ((t % 2) * ((t + 1) // 2) + (1 - t % 2) * (self.R - t // 2)) % self.R

    def barrier(self):
        sem = pltpu.get_barrier_semaphore()
        others = [self.dev(dx=dx, dy=dy) for dx in range(self.X) for dy in range(self.R) if dx or dy]
        others += [self.dev(dz=1), self.dev(dz=self.R - 1), self.sibling()]
        for other in others:
            pl.semaphore_signal(sem, inc=1, device_id=other, device_id_type=MESH)
        pl.semaphore_wait(sem, len(others))


def remote(src, dst, s_sem, r_sem, to):
    return pltpu.make_async_remote_copy(
        src_ref=src, dst_ref=dst, send_sem=s_sem, recv_sem=r_sem, device_id=to, device_id_type=MESH
    )


def dot(a, b, ca, cb):
    return lax.dot_general(a, b, (((ca,), (cb,)), ((), ())), preferred_element_type=jnp.float32)


def columns(g):
    return pl.ds(pl.multiple_of(g * HD, HD), HD)


def load_query(QD, DL, LS, n, b, g):
    rows, cols = pl.ds(2 * b, 2), columns(g)
    qv = QD[rows, n, 0, :, cols].reshape(QB, HD)
    dov = QD[rows, n, 1, :, cols].reshape(QB, HD)
    lse = LS[n, pl.ds(b * GROUP + g, 1), :]
    delta = DL[2 * b, n, pl.ds(g, 1), :] + DL[2 * b + 1, n, pl.ds(g, 1), :]
    return qv, dov, lse, delta


def grads(qv, dov, lse, delta, kv, vv, mask=None):
    prob = jnp.exp(dot(kv, qv, 1, 1) * SCALE - lse)
    if mask is not None:
        prob = jnp.where(mask, prob, 0.0)
    ds = (prob * (dot(vv, dov, 1, 1) - delta)).astype(jnp.bfloat16)
    pb = prob.astype(jnp.bfloat16)
    return dot(ds, kv, 0, 0), dot(ds, qv, 1, 0), dot(pb, dov, 1, 0)


def gather_kernel(
    R, X, q, do, o, k, v, ls, QD, KV, DL, LS, LI, dq0, dkv0, dl, do_v, o_v,
    ys, yr, ls_s, ls_r, loc, qs, qr, fs, fr, ds, dr, ks, kr, ms, mr,
):
    p = Place(R, X)
    K = R // 2
    H = R // 2
    x, y, z, c = p.x, p.y, p.z, p.c
    loads = [
        pltpu.make_async_copy(src, dst, loc.at[6 + i])
        for i, (src, dst) in enumerate(((do, do_v), (o, o_v)))
    ]
    for copy in loads:
        copy.start()
    p.barrier()

    def pieces(t):
        head = (y + p.far(t)) % R
        qcol = pl.ds(pl.multiple_of(head * WIDE, WIDE), WIDE)
        kcol = pl.ds(pl.multiple_of(head * HD, HD), HD)
        return (
            (k.at[:, kcol], KV.at[c, z, y, 0]),
            (v.at[:, kcol], KV.at[c, z, y, 1]),
            (q.at[:, qcol], QD.at[x, y, 0]),
            (do.at[:, qcol], QD.at[x, y, 1]),
            (dl.at[head], DL.at[x, y]),
        )

    def y_send(t, i):
        src, dst = pieces(t)[i]
        return remote(src, dst, ys.at[i, t], yr.at[i, y], p.dev(dy=p.far(t)))

    def y_wait(t, i):
        n = (y + p.far(t)) % R
        dst = (KV.at[c, z, n, 0], KV.at[c, z, n, 1], QD.at[x, n, 0], QD.at[x, n, 1], DL.at[x, n])[i]
        remote(dst, dst, ys.at[i, t], yr.at[i, n], p.dev(dy=p.far(t))).wait_recv()

    own = [pltpu.make_async_copy(src, dst, loc.at[i]) for i, (src, dst) in enumerate(pieces(0))]
    for copy in own[:4]:
        copy.start()

    def y_start(t, kinds):
        for i in kinds:
            y_send(t, i).start()

    y_start(1, (2, 3))
    y_start(2, (2, 3))

    @pl.loop(1, R)
    def _(t):
        y_start(t, (0, 1))

    def ls_send(i, dx):
        return remote(
            ls.at[i], LS.at[y], ls_s.at[i, dx], ls_r.at[y], p.at((x + dx) % X, 2 * x + i, z)
        )

    ls_home = y // 2 == x
    ls_own = pltpu.make_async_copy(ls.at[y % 2], LS.at[y], loc.at[5])

    def ls_each(act):
        for i in range(2):
            for dx in range(X):
                if dx:
                    act(ls_send(i, dx))
                else:
                    pl.when(y != 2 * x + i)(functools.partial(act, ls_send(i, dx)))

    ls_each(lambda copy: copy.start())
    pl.when(ls_home)(ls_own.start)

    at_head = lax.broadcasted_iota(jnp.int32, (8, HD), 0)
    picks = [(at_head == g).astype(jnp.bfloat16) for g in range(GROUP)]
    lane = lax.broadcasted_iota(jnp.int32, (8, QB), 1)
    here = (lane // KB) == x % 2

    for copy in loads:
        copy.wait()

    @pl.loop(0, R)
    def _(n):
        cols = pl.ds(pl.multiple_of(n * WIDE, WIDE), WIDE)
        prod = do_v[:, cols].astype(jnp.float32) * o_v[:, cols].astype(jnp.float32)
        high = prod.astype(jnp.bfloat16)
        low = (prod - high.astype(jnp.float32)).astype(jnp.bfloat16)
        tile = jnp.zeros((8, KB), jnp.float32)
        for g in range(GROUP):
            at = slice(g * HD, (g + 1) * HD)
            tile += dot(picks[g], high[:, at], 1, 1) + dot(picks[g], low[:, at], 1, 1)
        dl[n] = jnp.where(here, jnp.concatenate([tile, tile], axis=1), 0.0)

    own[4].start()

    @pl.loop(1, R)
    def _(t):
        y_start(t, (4,))

    @pl.loop(3, R)
    def _(t):
        y_start(t, (2, 3))

    def q_send(d, t):
        n = (y + p.far(t)) % R
        part = QD.at[x, n]
        return remote(part, part, qs.at[d, t], qr.at[d, t], p.dev(dx=1 if d == 0 else X - 1))

    def q_arrived(d, t):
        n = (y + p.far(t)) % R
        part = QD.at[(x + (X - 1 if d == 0 else 1)) % X, n]
        remote(part, part, qs.at[d, t], qr.at[d, t], p.dev(dx=1 if d == 0 else X - 1)).wait_recv()

    def f_send(d, t):
        n = (y + p.far(t)) % R
        part = QD.at[(x + (X - 1 if d == 0 else 1)) % X, n, d]
        return remote(part, part, fs.at[d, t], fr.at[d, t], p.dev(dx=1 if d == 0 else X - 1))

    def f_arrived(d, t):
        n = (y + p.far(t)) % R
        part = QD.at[(x + 2) % X, n, d]
        remote(part, part, fs.at[d, t], fr.at[d, t], p.dev(dx=1 if d == 0 else X - 1)).wait_recv()

    def d_send(d, hop):
        part = DL.at[(x + (0, X - 1 if d == 0 else 1)[hop]) % X]
        return remote(part, part, ds.at[d, hop], dr.at[d, hop], p.dev(dx=1 if d == 0 else X - 1))

    def d_arrived(d, hop):
        part = DL.at[(x + (X - 1 if d == 0 else 1, 2)[hop]) % X]
        remote(part, part, ds.at[d, hop], dr.at[d, hop], p.dev(dx=1 if d == 0 else X - 1)).wait_recv()

    def k_block(d, hops):
        return (z + (R - hops if d == 0 else hops)) % R

    def k_send(d, step, h):
        part = KV.at[c, k_block(d, step - 1), pl.ds(h * H, H)]
        return remote(part, part, ks.at[d, step - 1, h], kr.at[d, step - 1, h], p.dev(dz=1 if d == 0 else R - 1))

    def k_arrived(d, step, h):
        part = KV.at[c, k_block(d, step), pl.ds(h * H, H)]
        remote(
            part, part, ks.at[d, step - 1, h], kr.at[d, step - 1, h], p.dev(dz=1 if d == 0 else R - 1)
        ).wait_recv()

    def mirror(b):
        return remote(KV.at[c, b], KV.at[c, b], ms.at[b], mr.at[b], p.sibling())

    def mirrored(b):
        part = KV.at[1 - c, b]
        remote(part, part, ms.at[b], mr.at[b], p.sibling()).wait_recv()

    def k_first():
        own[0].wait()
        own[1].wait()

        @pl.loop(1, R)
        def _(t):
            y_wait(t, 0)
            y_wait(t, 1)

        for h in range(2):
            k_send(0, 1, h).start()
            k_send(1, 1, h).start()
        mirror(z).start()

    def k_step(step):
        for h in range(2):
            k_arrived(0, step - 1, h)
            if step < K or h == 0:
                k_send(0, step, h).start()
            k_arrived(1, step - 1, h)
            if step < K or h == 1:
                k_send(1, step, h).start()
        mirror(k_block(0, step - 1)).start()
        mirror(k_block(1, step - 1)).start()

    def spread(t):
        for d in range(2):
            q_send(d, t).start()

    def forward(t):
        for d in range(2):
            q_arrived(d, t)
            f_send(d, t).start()

    def d_first():
        own[4].wait()

        @pl.loop(1, R)
        def _(t):
            y_wait(t, 4)

        d_send(0, 0).start()
        d_send(1, 0).start()

    def d_second():
        d_arrived(0, 0)
        d_send(0, 1).start()
        d_arrived(1, 0)

    def stats_arrived():
        @pl.loop(1, R)
        def _(t):
            n = (y + t) % R
            remote(LS.at[n], LS.at[n], ls_s.at[0, 0], ls_r.at[n], p.dev(dy=1)).wait_recv()

        pl.when(ls_home)(ls_own.wait)

        @pl.when(jnp.logical_not(ls_home))
        def _():
            remote(LS.at[y], LS.at[y], ls_s.at[0, 0], ls_r.at[y], p.dev(dy=1)).wait_recv()

        LI[...] = LS[:, 2 * GROUP, :]

    key_at = lax.broadcasted_iota(jnp.int32, (KB, QB), 0) + (x % 2) * KB
    causal = key_at <= lax.broadcasted_iota(jnp.int32, (KB, QB), 1)

    def own_terms(t):
        n = (y + p.far(t)) % R
        kv, vv = KV[c, z, n, 0], KV[c, z, n, 1]
        results = [grads(*load_query(QD, DL, LS, n, x // 2, g), kv, vv, causal) for g in range(GROUP)]
        for g in range(GROUP):
            dq0[:, n, :, g * HD : (g + 1) * HD] = results[g][0].reshape(2, KB, HD)
        dkv0[n, 0] = sum(r[1] for r in results)
        dkv0[n, 1] = sum(r[2] for r in results)

    own[2].wait()
    own[3].wait()
    spread(0)
    for t in range(1, R):
        y_wait(t, 2)
        y_wait(t, 3)
        spread(t)
        if t > 1:
            forward(t - 2)
        if t == 1:
            k_first()
        if t == 2:
            d_first()
            stats_arrived()
        if t == 3:
            d_second()
        if t in (3, 5, 7):
            k_step((t + 1) // 2)
        if t >= 4:
            for e in ((0, 1), (2, 3), (4,), (5,))[t - 4]:
                own_terms(e)

    forward(R - 2)
    forward(R - 1)
    own_terms(R - 2)
    own_terms(R - 1)
    k_arrived(0, K, 0)
    k_arrived(1, K, 1)
    mirror(k_block(0, K)).start()

    @pl.loop(0, R)
    def _(t):
        f_arrived(0, t)
        f_arrived(1, t)

    d_arrived(0, 1)

    @pl.loop(0, R)
    def _(b):
        mirrored(b)

    ls_each(lambda copy: copy.wait_send())

    @pl.loop(1, R)
    def _(t):
        for i in range(5):
            y_send(t, i).wait_send()

    @pl.loop(0, R)
    def _(t):
        for d in range(2):
            q_send(d, t).wait_send()
            f_send(d, t).wait_send()
        mirror(t).wait_send()

    d_send(0, 0).wait_send()
    d_send(1, 0).wait_send()
    d_send(0, 1).wait_send()
    for step in range(1, K + 1):
        for h in range(2):
            if step < K or h == 0:
                k_send(0, step, h).wait_send()
            if step < K or h == 1:
                k_send(1, step, h).wait_send()


def gather(R, X, q, do, o, k, v, ls):
    K = R // 2
    rows = q.shape[0]
    anyspace = pl.BlockSpec(memory_space=pl.ANY)
    vmem = pl.BlockSpec(memory_space=pltpu.VMEM)
    dma = pltpu.SemaphoreType.DMA
    f32 = jnp.float32
    return pl.pallas_call(
        functools.partial(gather_kernel, R, X),
        out_shape=(
            jax.ShapeDtypeStruct((X, R, 2, rows, WIDE), jnp.bfloat16),
            jax.ShapeDtypeStruct((2, R, R, 2, rows, HD), jnp.bfloat16),
            jax.ShapeDtypeStruct((X, R, 8, QB), f32),
            jax.ShapeDtypeStruct((R,) + ls.shape[1:], f32),
            jax.ShapeDtypeStruct((R, QB), f32),
            jax.ShapeDtypeStruct((2, R, rows, WIDE), f32),
            jax.ShapeDtypeStruct((R, 2, rows, HD), f32),
        ),
        in_specs=[pl.BlockSpec(memory_space=pltpu.HBM)] * 5 + [anyspace],
        out_specs=(vmem,) * 7,
        scratch_shapes=[
            pltpu.VMEM((R, 8, QB), f32),
            pltpu.VMEM(do.shape, do.dtype),
            pltpu.VMEM(o.shape, o.dtype),
            dma((5, R)),
            dma((5, R)),
            dma((2, X)),
            dma((R,)),
            dma((8,)),
            dma((2, R)),
            dma((2, R)),
            dma((2, R)),
            dma((2, R)),
            dma((2, 2)),
            dma((2, 2)),
            dma((2, K, 2)),
            dma((2, K, 2)),
            dma((R,)),
            dma((R,)),
        ],
        compiler_params=pltpu.CompilerParams(
            collective_id=1, has_side_effects=True, vmem_limit_bytes=20 << 20
        ),
        name="gather_rings",
    )(q, do, o, k, v, ls)


def pair_kernel(LI, QD, KV, DL, LS, dq0, dkv0, dq, dkv, pairs):
    X, R = QD.shape[:2]
    x = lax.axis_index("head")
    s = lax.axis_index("seq")
    c, z = s % 2, (s // 2) % R
    own_b = x // 2
    blocks = 2 * R * R
    listed = GROUP * NSEL

    def scan(i, count):
        dq[i // R, i % R] = jnp.zeros(dq.shape[2:], jnp.float32)
        for e in range(blocks // (X * R)):
            dkv[i * (blocks // (X * R)) + e] = jnp.zeros(dkv.shape[1:], jnp.float32)
        for e in range(2 * R * listed // (X * R)):
            k = i * (2 * R * listed // (X * R)) + e
            block = LI[k // (2 * listed), k % (2 * listed)].astype(jnp.int32)
            shard = block // X
            key = ((shard % 2) * R + shard // 2 % R) * R + shard // (2 * R)
            pairs[count] = (k // NSEL) * blocks + key
            count += (block % X == x).astype(jnp.int32)
        return count

    count = lax.fori_loop(0, X * R, scan, jnp.int32(0))
    for e in range(UNROLL):
        pairs[count + e] = 0

    @pl.loop(0, R)
    def _(n):
        dq[pl.ds(2 * own_b, 2), n] = dq0[:, n]
        dkv[(c * R + z) * R + n] = dkv0[n]

    @pl.loop(0, (count + UNROLL - 1) // UNROLL)
    def _(t):
        results = []
        for u in range(UNROLL):
            i = t * UNROLL + u
            code = pairs[i]
            unit, key = code // blocks, code % blocks
            g, b, n = unit % GROUP, unit // GROUP % 2, unit // (2 * GROUP)
            qv, dov, lse, delta = load_query(QD, DL, LS, n, b, g)
            lse = lse + jnp.where(i < count, 0.0, 1e30)
            results.append((n, b, g, key, grads(qv, dov, lse, delta, KV[key, 0], KV[key, 1])))
        for n, b, g, key, out in results:
            dq[pl.ds(2 * b, 2), n, :, columns(g)] += out[0].reshape(2, KB, HD)
            dkv[key, 0] += out[1]
            dkv[key, 1] += out[2]


def pair_grads(LI, QD, KV, DL, LS, dq0, dkv0):
    vmem = pl.BlockSpec(memory_space=pltpu.VMEM)
    smem = pl.BlockSpec(memory_space=pltpu.SMEM)
    X, R = QD.shape[:2]
    flat = KV.reshape((2 * R * R,) + KV.shape[3:])
    dq, dkv = pl.pallas_call(
        pair_kernel,
        out_shape=(
            jax.ShapeDtypeStruct(QD.shape[:2] + QD.shape[3:], jnp.float32),
            jax.ShapeDtypeStruct(flat.shape, jnp.float32),
        ),
        in_specs=[smem] + [vmem] * 6,
        out_specs=(vmem,) * 2,
        scratch_shapes=[pltpu.SMEM((2 * R * GROUP * NSEL + UNROLL,), jnp.int32)],
        compiler_params=pltpu.CompilerParams(vmem_limit_bytes=28 << 20),
        name="pair_grads",
    )(LI, QD, flat, DL, LS, dq0, dkv0)
    return dq, dkv.reshape(KV.shape)


def reduce_kernel(
    R, X, dq, dkv, gq, gk, gv, sf, sp, fq, rq, sm, mk, rk, bq, bk,
    ys, yr, loc, fs, fr, qs, qr, ms, mr, ks, kr,
):
    p = Place(R, X)
    K = R // 2
    H = R // 2
    x, y, z, c = p.x, p.y, p.z, p.c
    rows = dq.shape[2]
    half = rows // 2
    p.barrier()
    f32 = jnp.float32

    def piece(t):
        return (y + p.far(R - 1 - t)) % R

    def x_to(d):
        return p.dev(dx=1 if d == 0 else X - 1)

    def z_to(d):
        return p.dev(dz=1 if d == 0 else R - 1)

    def part_q(dx, n, at=slice(None)):
        return dq[(x + dx) % X, n, at] * SCALE

    def part_kv(core, b, at=slice(None)):
        part = dkv[core, b, at]
        return jnp.concatenate([part[:, :1] * SCALE, part[:, 1:]], axis=1)

    def f_send(d, t):
        return remote(sf.at[d, t], fq.at[d, t], fs.at[d, t], fr.at[d, t], x_to(d))

    def f_start(t):
        for d in range(2):
            sf[d, t] = part_q(2, piece(t), pl.ds(d * half, half)).astype(jnp.bfloat16)
            f_send(d, t).start()

    def q_send(d, t, late):
        src = (fq if late else sp).at[d, t]
        dst = rq.at[d, t, pl.ds((d if late else 1 - d) * half, half)]
        return remote(src, dst, qs.at[late, d, t], qr.at[late, d, t], x_to(d))

    def q_plain(t):
        for d in range(2):
            at = pl.ds((1 - d) * half, half)
            sp[d, t] = part_q(1 if d == 0 else X - 1, piece(t), at).astype(jnp.bfloat16)
            q_send(d, t, 0).start()

    def q_add(t):
        q_plain(t)
        for d in range(2):
            f_send(d, t).wait_recv()
            mine = part_q(1 if d == 0 else X - 1, piece(t), pl.ds(d * half, half))
            fq[d, t] = (mine + fq[d, t].astype(f32)).astype(jnp.bfloat16)
            q_send(d, t, 1).start()

    def mirror(b):
        return remote(sm.at[b], mk.at[b], ms.at[b], mr.at[b], p.sibling())

    def m_start(b):
        sm[b] = part_kv(1 - c, b).astype(jnp.bfloat16)
        mirror(b).start()

    def owner(d, step):
        far = K + 1 - step
        return (z + (far if d == 0 else R - far)) % R

    def k_send(d, step, h):
        src = mk.at[owner(d, step), pl.ds(h * H, H)]
        return remote(src, rk.at[d, step - 1, h], ks.at[d, step - 1, h], kr.at[d, step - 1, h], z_to(d))

    def k_step(step):
        for d in range(2):
            b = owner(d, step)
            if step > 1 or d == 0:
                mirror(b).wait_recv()
            for h in range(2):
                if step == 1 and h != d:
                    continue
                at = pl.ds(h * H, H)
                total = mk[b, at].astype(f32) + part_kv(c, b, at)
                if step > 2 or (step == 2 and h == d):
                    k_send(d, step - 1, h).wait_recv()
                    total = total + rk[d, step - 2, h].astype(f32)
                mk[b, at] = total.astype(jnp.bfloat16)
                k_send(d, step, h).start()

    m_start((z + K) % R)
    pl.loop(0, R)(f_start)
    for far in range(K - 1, 0, -1):
        m_start((z + far) % R)
        m_start((z + R - far) % R)
    m_start(z)

    def out_refs(n, head):
        qcol = pl.ds(pl.multiple_of(head * WIDE, WIDE), WIDE)
        kcol = pl.ds(pl.multiple_of(head * HD, HD), HD)
        return (
            (bq.at[n], gq.at[:, qcol]),
            (bk.at[n, 0], gk.at[:, kcol]),
            (bk.at[n, 1], gv.at[:, kcol]),
        )

    def y_send(t, i):
        src, dst = out_refs(piece(t), y)[i]
        return remote(src, dst, ys.at[i, t], yr.at[i, y], p.dev(dy=p.far(R - 1 - t)))

    def y_wait(t, i):
        n = piece(t)
        src, dst = out_refs(n, n)[i]
        remote(src, dst, ys.at[i, t], yr.at[i, n], p.dev(dy=p.far(R - 1 - t))).wait_recv()

    own = [pltpu.make_async_copy(src, dst, loc.at[i]) for i, (src, dst) in enumerate(out_refs(y, y))]

    def q_total(t):
        for d in range(2):
            q_send(d, t, 0).wait_recv()
            q_send(d, t, 1).wait_recv()
        n = piece(t)
        bq[n] = (part_q(0, n) + rq[0, t].astype(f32) + rq[1, t].astype(f32)).astype(jnp.bfloat16)

    def q_home(t):
        q_total(t)
        y_send(t, 0).start()

    k_step(1)
    pl.loop(0, H)(q_add)
    k_step(2)
    pl.loop(H, R)(q_add)
    k_step(3)
    pl.loop(0, H)(q_home)
    for step in range(4, K + 1):
        k_step(step)
    pl.loop(H, R - 1)(q_home)
    q_total(R - 1)
    own[0].start()
    mirror(z).wait_recv()
    for h in range(2):
        at = pl.ds(h * H, H)
        total = part_kv(c, z, at) + mk[z, at].astype(f32)
        for d in range(2):
            k_send(d, K, h).wait_recv()
            total = total + rk[d, K - 1, h].astype(f32)
        bk[at] = total.astype(jnp.bfloat16)

    @pl.loop(0, R - 1)
    def _(t):
        y_send(t, 1).start()
        y_send(t, 2).start()

    own[1].start()
    own[2].start()

    @pl.loop(0, R - 1)
    def _(t):
        for i in range(3):
            y_wait(t, i)

    for copy in own:
        copy.wait()

    @pl.loop(0, R - 1)
    def _(t):
        for i in range(3):
            y_send(t, i).wait_send()

    @pl.loop(0, R)
    def _(t):
        for d in range(2):
            f_send(d, t).wait_send()
            q_send(d, t, 0).wait_send()
            q_send(d, t, 1).wait_send()
        mirror(t).wait_send()

    for step in range(1, K + 1):
        for h in range(2):
            for d in range(2):
                if step > 1 or h == d:
                    k_send(d, step, h).wait_send()


def reduce(R, X, dq, dkv):
    K = R // 2
    rows = dq.shape[2]
    anyspace = pl.BlockSpec(memory_space=pl.ANY)
    vmem = pl.BlockSpec(memory_space=pltpu.VMEM)
    dma = pltpu.SemaphoreType.DMA
    bf16 = jnp.bfloat16
    return pl.pallas_call(
        functools.partial(reduce_kernel, R, X),
        out_shape=(
            jax.ShapeDtypeStruct((rows, R * WIDE), bf16),
            jax.ShapeDtypeStruct((rows, R * HD), bf16),
            jax.ShapeDtypeStruct((rows, R * HD), bf16),
        ),
        in_specs=[vmem] * 2,
        out_specs=(anyspace,) * 3,
        scratch_shapes=[
            pltpu.VMEM((2, R, rows // 2, WIDE), bf16),
            pltpu.VMEM((2, R, rows // 2, WIDE), bf16),
            pltpu.VMEM((2, R, rows // 2, WIDE), bf16),
            pltpu.VMEM((2, R, rows, WIDE), bf16),
            pltpu.VMEM(dkv.shape[1:], bf16),
            pltpu.VMEM(dkv.shape[1:], bf16),
            pltpu.VMEM((2, K, 2, R // 2) + dkv.shape[3:], bf16),
            pltpu.VMEM(dq.shape[1:], bf16),
            pltpu.VMEM(dkv.shape[2:], bf16),
            dma((3, R)),
            dma((3, R)),
            dma((3,)),
            dma((2, R)),
            dma((2, R)),
            dma((2, 2, R)),
            dma((2, 2, R)),
            dma((R,)),
            dma((R,)),
            dma((2, K, 2)),
            dma((2, K, 2)),
        ],
        compiler_params=pltpu.CompilerParams(
            collective_id=2, has_side_effects=True, vmem_limit_bytes=26 << 20
        ),
        name="reduce_rings",
    )(dq, dkv)


def body(R, X, queries, keys, values, outputs_saved, grad_out, lse, block_lists):
    stats = lse.reshape(2, QB, 2, GROUP).transpose(2, 0, 3, 1).reshape(2, 2 * GROUP, QB)
    lists = lax.dynamic_slice_in_dim(block_lists, 2 * lax.axis_index("seq"), 2, 0)
    lists = lists.reshape(2, 2, GROUP, NSEL).transpose(1, 0, 2, 3).reshape(2, 1, 2 * GROUP * NSEL)
    lists = jnp.pad(lists.astype(jnp.float32), ((0, 0), (0, 7), (0, QB - 2 * GROUP * NSEL)))
    stats = jnp.concatenate([stats, lists], axis=1)
    QD, KV, DL, LS, LI, dq0, dkv0 = gather(
        R, X, queries, grad_out, outputs_saved, keys, values, stats
    )
    dq, dkv = pair_grads(LI, QD, KV, DL, LS, dq0, dkv0)
    return reduce(R, X, dq, dkv)


def solution(mesh):
    R = math.isqrt(mesh.shape["seq"] // 2)
    X = mesh.shape["head"]
    in_specs = (
        P(("seq", "head"), None),
        P(("seq", "head"), None),
        P(("seq", "head"), None),
        P(("seq", "head"), None),
        P(("seq", "head"), None),
        P("seq", "head"),
        P(None, "head", None),
    )
    out_specs = (P(("seq", "head"), None), P(("seq", "head"), None), P(("seq", "head"), None))
    return jax.shard_map(
        functools.partial(body, R, X), mesh=mesh, in_specs=in_specs, out_specs=out_specs, check_vma=False
    )
```

```python
import functools
import math

import jax
import jax.numpy as jnp
from jax import lax
from jax.experimental import pallas as pl
from jax.experimental.pallas import tpu as pltpu
from jax.sharding import PartitionSpec as P

HD = 128
QB = 128
KB = 64
NSEL = 4
GROUP = 4
WIDE = GROUP * HD
MESH = pl.DeviceIdType.MESH
SCALE = HD ** (-0.5)
UNROLL = 4
PARTS = 4


class Place:
    def __init__(self, R, X):
        self.R, self.X = R, X
        self.x = lax.axis_index("head")
        s = lax.axis_index("seq")
        self.c = s % 2
        self.z = (s // 2) % R
        self.y = s // (2 * R)

    def dev(self, dx=0, dy=0, dz=0):
        return self.at((self.x + dx) % self.X, (self.y + dy) % self.R, (self.z + dz) % self.R)

    def at(self, x, y, z):
        return ((y * self.R + z) * 2 + self.c, x)

    def sibling(self):
        return ((self.y * self.R + self.z) * 2 + 1 - self.c, self.x)

    def far(self, t):
        return ((t % 2) * ((t + 1) // 2) + (1 - t % 2) * (self.R - t // 2)) % self.R

    def barrier(self):
        sem = pltpu.get_barrier_semaphore()
        others = [self.dev(dx=dx, dy=dy) for dx in range(self.X) for dy in range(self.R) if dx or dy]
        others += [self.dev(dz=1), self.dev(dz=self.R - 1), self.sibling()]
        for other in others:
            pl.semaphore_signal(sem, inc=1, device_id=other, device_id_type=MESH)
        pl.semaphore_wait(sem, len(others))


def remote(src, dst, s_sem, r_sem, to):
    return pltpu.make_async_remote_copy(
        src_ref=src, dst_ref=dst, send_sem=s_sem, recv_sem=r_sem, device_id=to, device_id_type=MESH
    )


def dot(a, b, ca, cb):
    return lax.dot_general(a, b, (((ca,), (cb,)), ((), ())), preferred_element_type=jnp.float32)


def quot(a, n):
    return lax.shift_right_logical(a, jnp.int32(n.bit_length() - 1))


def rest(a, n):
    return a & jnp.int32(n - 1)


def columns(g):
    return pl.ds(pl.multiple_of(g * HD, HD), HD)


def load_query(QD, DL, LS, n, b, g):
    rows, cols = pl.ds(2 * b, 2), columns(g)
    qv = QD[rows, n, 0, :, cols].reshape(QB, HD)
    dov = QD[rows, n, 1, :, cols].reshape(QB, HD)
    lse = LS[n, pl.ds(b * GROUP + g, 1), :]
    delta = DL[2 * b, n, pl.ds(g, 1), :] + DL[2 * b + 1, n, pl.ds(g, 1), :]
    return qv, dov, lse, delta


def grads(qv, dov, lse, delta, kv, vv, mask=None):
    both = dot(jnp.concatenate([kv, vv], axis=0), jnp.concatenate([qv, dov], axis=0), 1, 1)
    prob = jnp.exp(both[:KB, :QB] * SCALE - lse)
    if mask is not None:
        prob = jnp.where(mask, prob, 0.0)
    ds = (prob * (both[KB:, QB:] - delta)).astype(jnp.bfloat16)
    pb = prob.astype(jnp.bfloat16)
    return dot(ds, kv, 0, 0), dot(ds, qv, 1, 0), dot(pb, dov, 1, 0)


def gather_kernel(
    R, X, q, do, o, k, v, ls, QD, KV, DL, LS, LI, dq0, dkv0, dl, do_v, o_v,
    ys, yr, ls_s, ls_r, loc, qs, qr, fs, fr, ds, dr, ks, kr, ms, mr,
):
    p = Place(R, X)
    K = R // 2
    H = R // 2
    x, y, z, c = p.x, p.y, p.z, p.c
    loads = [
        pltpu.make_async_copy(src, dst, loc.at[6 + i])
        for i, (src, dst) in enumerate(((do, do_v), (o, o_v)))
    ]
    for copy in loads:
        copy.start()
    p.barrier()

    def pieces(t):
        head = (y + p.far(t)) % R
        qcol = pl.ds(pl.multiple_of(head * WIDE, WIDE), WIDE)
        kcol = pl.ds(pl.multiple_of(head * HD, HD), HD)
        return (
            (k.at[:, kcol], KV.at[c, z, y, 0]),
            (v.at[:, kcol], KV.at[c, z, y, 1]),
            (q.at[:, qcol], QD.at[x, y, 0]),
            (do.at[:, qcol], QD.at[x, y, 1]),
            (dl.at[head], DL.at[x, y]),
        )

    def y_send(t, i):
        src, dst = pieces(t)[i]
        return remote(src, dst, ys.at[i, t], yr.at[i, y], p.dev(dy=p.far(t)))

    def y_wait(t, i):
        n = (y + p.far(t)) % R
        dst = (KV.at[c, z, n, 0], KV.at[c, z, n, 1], QD.at[x, n, 0], QD.at[x, n, 1], DL.at[x, n])[i]
        remote(dst, dst, ys.at[i, t], yr.at[i, n], p.dev(dy=p.far(t))).wait_recv()

    own = [pltpu.make_async_copy(src, dst, loc.at[i]) for i, (src, dst) in enumerate(pieces(0))]
    for copy in own[:4]:
        copy.start()

    def y_start(t, kinds):
        for i in kinds:
            y_send(t, i).start()

    y_start(1, (2, 3))
    y_start(2, (2, 3))

    @pl.loop(1, R)
    def _(t):
        y_start(t, (0, 1))

    def ls_send(i, dx):
        return remote(
            ls.at[i], LS.at[y], ls_s.at[i, dx], ls_r.at[y], p.at((x + dx) % X, 2 * x + i, z)
        )

    ls_home = y // 2 == x
    ls_own = pltpu.make_async_copy(ls.at[y % 2], LS.at[y], loc.at[5])

    def ls_each(act):
        for i in range(2):
            for dx in range(X):
                if dx:
                    act(ls_send(i, dx))
                else:
                    pl.when(y != 2 * x + i)(functools.partial(act, ls_send(i, dx)))

    ls_each(lambda copy: copy.start())
    pl.when(ls_home)(ls_own.start)

    at_head = lax.broadcasted_iota(jnp.int32, (8, HD), 0)
    picks = [(at_head == g).astype(jnp.bfloat16) for g in range(GROUP)]
    lane = lax.broadcasted_iota(jnp.int32, (8, QB), 1)
    here = (lane // KB) == x % 2

    for copy in loads:
        copy.wait()

    @pl.loop(0, R)
    def _(n):
        cols = pl.ds(pl.multiple_of(n * WIDE, WIDE), WIDE)
        prod = do_v[:, cols].astype(jnp.float32) * o_v[:, cols].astype(jnp.float32)
        high = prod.astype(jnp.bfloat16)
        low = (prod - high.astype(jnp.float32)).astype(jnp.bfloat16)
        tile = jnp.zeros((8, KB), jnp.float32)
        for g in range(GROUP):
            at = slice(g * HD, (g + 1) * HD)
            tile += dot(picks[g], high[:, at], 1, 1) + dot(picks[g], low[:, at], 1, 1)
        dl[n] = jnp.where(here, jnp.concatenate([tile, tile], axis=1), 0.0)

    own[4].start()

    @pl.loop(1, R)
    def _(t):
        y_start(t, (4,))

    @pl.loop(3, R)
    def _(t):
        y_start(t, (2, 3))

    def q_send(d, t):
        n = (y + p.far(t)) % R
        part = QD.at[x, n]
        return remote(part, part, qs.at[d, t], qr.at[d, t], p.dev(dx=1 if d == 0 else X - 1))

    def q_arrived(d, t):
        n = (y + p.far(t)) % R
        part = QD.at[(x + (X - 1 if d == 0 else 1)) % X, n]
        remote(part, part, qs.at[d, t], qr.at[d, t], p.dev(dx=1 if d == 0 else X - 1)).wait_recv()

    def f_send(d, t):
        n = (y + p.far(t)) % R
        part = QD.at[(x + (X - 1 if d == 0 else 1)) % X, n, d]
        return remote(part, part, fs.at[d, t], fr.at[d, t], p.dev(dx=1 if d == 0 else X - 1))

    def f_arrived(d, t):
        n = (y + p.far(t)) % R
        part = QD.at[(x + 2) % X, n, d]
        remote(part, part, fs.at[d, t], fr.at[d, t], p.dev(dx=1 if d == 0 else X - 1)).wait_recv()

    def d_send(d, hop):
        part = DL.at[(x + (0, X - 1 if d == 0 else 1)[hop]) % X]
        return remote(part, part, ds.at[d, hop], dr.at[d, hop], p.dev(dx=1 if d == 0 else X - 1))

    def d_arrived(d, hop):
        part = DL.at[(x + (X - 1 if d == 0 else 1, 2)[hop]) % X]
        remote(part, part, ds.at[d, hop], dr.at[d, hop], p.dev(dx=1 if d == 0 else X - 1)).wait_recv()

    def k_block(d, hops):
        return (z + (R - hops if d == 0 else hops)) % R

    def k_send(d, step, h):
        part = KV.at[c, k_block(d, step - 1), pl.ds(h * H, H)]
        return remote(part, part, ks.at[d, step - 1, h], kr.at[d, step - 1, h], p.dev(dz=1 if d == 0 else R - 1))

    def k_arrived(d, step, h):
        part = KV.at[c, k_block(d, step), pl.ds(h * H, H)]
        remote(
            part, part, ks.at[d, step - 1, h], kr.at[d, step - 1, h], p.dev(dz=1 if d == 0 else R - 1)
        ).wait_recv()

    def mirror(b):
        return remote(KV.at[c, b], KV.at[c, b], ms.at[b], mr.at[b], p.sibling())

    def mirrored(b):
        part = KV.at[1 - c, b]
        remote(part, part, ms.at[b], mr.at[b], p.sibling()).wait_recv()

    def k_first():
        own[0].wait()
        own[1].wait()

        @pl.loop(1, R)
        def _(t):
            y_wait(t, 0)
            y_wait(t, 1)

        for h in range(2):
            k_send(0, 1, h).start()
            k_send(1, 1, h).start()
        mirror(z).start()

    def k_step(step):
        for h in range(2):
            k_arrived(0, step - 1, h)
            if step < K or h == 0:
                k_send(0, step, h).start()
            k_arrived(1, step - 1, h)
            if step < K or h == 1:
                k_send(1, step, h).start()
        mirror(k_block(0, step - 1)).start()
        mirror(k_block(1, step - 1)).start()

    def spread(t):
        for d in range(2):
            q_send(d, t).start()

    def forward(t):
        for d in range(2):
            q_arrived(d, t)
            f_send(d, t).start()

    def d_first():
        own[4].wait()

        @pl.loop(1, R)
        def _(t):
            y_wait(t, 4)

        d_send(0, 0).start()
        d_send(1, 0).start()

    def d_second():
        d_arrived(0, 0)
        d_send(0, 1).start()
        d_arrived(1, 0)

    def stats_arrived():
        @pl.loop(1, R)
        def _(t):
            n = (y + t) % R
            remote(LS.at[n], LS.at[n], ls_s.at[0, 0], ls_r.at[n], p.dev(dy=1)).wait_recv()

        pl.when(ls_home)(ls_own.wait)

        @pl.when(jnp.logical_not(ls_home))
        def _():
            remote(LS.at[y], LS.at[y], ls_s.at[0, 0], ls_r.at[y], p.dev(dy=1)).wait_recv()

        LI[...] = LS[:, 2 * GROUP, :]

    key_at = lax.broadcasted_iota(jnp.int32, (KB, QB), 0) + (x % 2) * KB
    causal = key_at <= lax.broadcasted_iota(jnp.int32, (KB, QB), 1)

    def own_terms(t):
        n = (y + p.far(t)) % R
        kv, vv = KV[c, z, n, 0], KV[c, z, n, 1]
        results = [grads(*load_query(QD, DL, LS, n, x // 2, g), kv, vv, causal) for g in range(GROUP)]
        for g in range(GROUP):
            dq0[:, n, :, g * HD : (g + 1) * HD] = results[g][0].reshape(2, KB, HD)
        dkv0[n, 0] = sum(r[1] for r in results)
        dkv0[n, 1] = sum(r[2] for r in results)

    own[2].wait()
    own[3].wait()
    spread(0)
    for t in range(1, R):
        y_wait(t, 2)
        y_wait(t, 3)
        spread(t)
        if t > 1:
            forward(t - 2)
        if t == 1:
            k_first()
        if t == 2:
            d_first()
            stats_arrived()
        if t == 3:
            d_second()
        if t in (3, 5, 7):
            k_step((t + 1) // 2)
        if t >= 4:
            for e in ((0, 1), (2, 3), (4,), (5,))[t - 4]:
                own_terms(e)

    forward(R - 2)
    forward(R - 1)
    own_terms(R - 2)
    own_terms(R - 1)
    k_arrived(0, K, 0)
    k_arrived(1, K, 1)
    mirror(k_block(0, K)).start()

    @pl.loop(0, R)
    def _(t):
        f_arrived(0, t)
        f_arrived(1, t)

    d_arrived(0, 1)

    @pl.loop(0, R)
    def _(b):
        mirrored(b)

    ls_each(lambda copy: copy.wait_send())

    @pl.loop(1, R)
    def _(t):
        for i in range(5):
            y_send(t, i).wait_send()

    @pl.loop(0, R)
    def _(t):
        for d in range(2):
            q_send(d, t).wait_send()
            f_send(d, t).wait_send()
        mirror(t).wait_send()

    d_send(0, 0).wait_send()
    d_send(1, 0).wait_send()
    d_send(0, 1).wait_send()
    for step in range(1, K + 1):
        for h in range(2):
            if step < K or h == 0:
                k_send(0, step, h).wait_send()
            if step < K or h == 1:
                k_send(1, step, h).wait_send()


def gather(R, X, q, do, o, k, v, ls):
    K = R // 2
    rows = q.shape[0]
    anyspace = pl.BlockSpec(memory_space=pl.ANY)
    vmem = pl.BlockSpec(memory_space=pltpu.VMEM)
    dma = pltpu.SemaphoreType.DMA
    f32 = jnp.float32
    return pl.pallas_call(
        functools.partial(gather_kernel, R, X),
        out_shape=(
            jax.ShapeDtypeStruct((X, R, 2, rows, WIDE), jnp.bfloat16),
            jax.ShapeDtypeStruct((2, R, R, 2, rows, HD), jnp.bfloat16),
            jax.ShapeDtypeStruct((X, R, 8, QB), f32),
            jax.ShapeDtypeStruct((R,) + ls.shape[1:], f32),
            jax.ShapeDtypeStruct((R, QB), f32),
            jax.ShapeDtypeStruct((2, R, rows, WIDE), f32),
            jax.ShapeDtypeStruct((R, 2, rows, HD), f32),
        ),
        in_specs=[anyspace] * 6,
        out_specs=(vmem,) * 7,
        scratch_shapes=[
            pltpu.VMEM((R, 8, QB), f32),
            pltpu.VMEM(do.shape, do.dtype),
            pltpu.VMEM(o.shape, o.dtype),
            dma((5, R)),
            dma((5, R)),
            dma((2, X)),
            dma((R,)),
            dma((8,)),
            dma((2, R)),
            dma((2, R)),
            dma((2, R)),
            dma((2, R)),
            dma((2, 2)),
            dma((2, 2)),
            dma((2, K, 2)),
            dma((2, K, 2)),
            dma((R,)),
            dma((R,)),
        ],
        compiler_params=pltpu.CompilerParams(
            collective_id=1, has_side_effects=True, vmem_limit_bytes=20 << 20
        ),
        name="gather_rings",
    )(*(pltpu.with_memory_space_constraint(a, pltpu.HBM) for a in (q, do, o, k, v)), ls)


def pair_kernel(LI, QD, KV, DL, LS, dq0, dkv0, dq, dkv, pairs):
    X, R = QD.shape[:2]
    x = lax.axis_index("head")
    s = lax.axis_index("seq")
    c, z = s % 2, (s // 2) % R
    own_b = x // 2
    blocks = 2 * R * R
    listed = GROUP * NSEL

    def scan(i, count):
        dq[i // R, i % R] = jnp.zeros(dq.shape[2:], jnp.float32)
        for e in range(blocks // (X * R)):
            dkv[i * (blocks // (X * R)) + e] = jnp.zeros(dkv.shape[1:], jnp.float32)
        for e in range(2 * R * listed // (X * R)):
            k = i * (2 * R * listed // (X * R)) + e
            block = LI[quot(k, 2 * listed), rest(k, 2 * listed)].astype(jnp.int32)
            shard = quot(block, X)
            key = (rest(shard, 2) * R + rest(quot(shard, 2), R)) * R + quot(shard, 2 * R)
            pairs[count] = quot(k, NSEL) * blocks + key
            count += (rest(block, X) == x).astype(jnp.int32)
        return count

    count = lax.fori_loop(0, X * R, scan, jnp.int32(0))
    for e in range(UNROLL):
        pairs[count + e] = 0

    @pl.loop(0, R)
    def _(n):
        dq[pl.ds(2 * own_b, 2), n] = dq0[:, n]
        dkv[(c * R + z) * R + n] = dkv0[n]

    @pl.loop(0, (count + UNROLL - 1) // UNROLL)
    def _(t):
        results = []
        for u in range(UNROLL):
            i = t * UNROLL + u
            code = pairs[i]
            unit, key = quot(code, blocks), rest(code, blocks)
            g, b, n = rest(unit, GROUP), rest(quot(unit, GROUP), 2), quot(unit, 2 * GROUP)
            qv, dov, lse, delta = load_query(QD, DL, LS, n, b, g)
            lse = lse + jnp.where(i < count, 0.0, 1e30)
            results.append((n, b, g, key, grads(qv, dov, lse, delta, KV[key, 0], KV[key, 1])))
        for n, b, g, key, out in results:
            dq[pl.ds(2 * b, 2), n, :, columns(g)] += out[0].reshape(2, KB, HD)
            dkv[key, 0] += out[1]
            dkv[key, 1] += out[2]


def pair_grads(LI, QD, KV, DL, LS, dq0, dkv0):
    vmem = pl.BlockSpec(memory_space=pltpu.VMEM)
    smem = pl.BlockSpec(memory_space=pltpu.SMEM)
    X, R = QD.shape[:2]
    flat = KV.reshape((2 * R * R,) + KV.shape[3:])
    dq, dkv = pl.pallas_call(
        pair_kernel,
        out_shape=(
            jax.ShapeDtypeStruct(QD.shape[:2] + QD.shape[3:], jnp.float32),
            jax.ShapeDtypeStruct(flat.shape, jnp.float32),
        ),
        in_specs=[smem] + [vmem] * 6,
        out_specs=(vmem,) * 2,
        scratch_shapes=[pltpu.SMEM((2 * R * GROUP * NSEL + UNROLL,), jnp.int32)],
        compiler_params=pltpu.CompilerParams(vmem_limit_bytes=28 << 20),
        name="pair_grads",
    )(LI, QD, flat, DL, LS, dq0, dkv0)
    return dq, dkv.reshape(KV.shape)


def reduce_kernel(
    R, X, dq, dkv, gq, gk, gv, sf, sp, fq, rq, sm, mk, rk, bq, bk,
    ys, yr, loc, fs, fr, qs, qr, ms, mr, ks, kr,
):
    p = Place(R, X)
    K = R // 2
    H = R // PARTS
    x, y, z, c = p.x, p.y, p.z, p.c
    rows = dq.shape[2]
    half = rows // 2
    p.barrier()
    f32 = jnp.float32

    def piece(t):
        return (y + p.far(R - 1 - t)) % R

    def x_to(d):
        return p.dev(dx=1 if d == 0 else X - 1)

    def z_to(d):
        return p.dev(dz=1 if d == 0 else R - 1)

    def part_q(dx, n, at=slice(None)):
        return dq[(x + dx) % X, n, at] * SCALE

    def part_kv(core, b, at=slice(None)):
        part = dkv[core, b, at]
        return jnp.concatenate([part[:, :1] * SCALE, part[:, 1:]], axis=1)

    def f_send(d, t):
        return remote(sf.at[d, t], fq.at[d, t], fs.at[d, t], fr.at[d, t], x_to(d))

    def f_start(t):
        for d in range(2):
            sf[d, t] = part_q(2, piece(t), pl.ds(d * half, half)).astype(jnp.bfloat16)
            f_send(d, t).start()

    def q_send(d, t, late):
        src = (fq if late else sp).at[d, t]
        dst = rq.at[d, t, pl.ds((d if late else 1 - d) * half, half)]
        return remote(src, dst, qs.at[late, d, t], qr.at[late, d, t], x_to(d))

    def q_plain(t):
        for d in range(2):
            at = pl.ds((1 - d) * half, half)
            sp[d, t] = part_q(1 if d == 0 else X - 1, piece(t), at).astype(jnp.bfloat16)
            q_send(d, t, 0).start()

    def q_add(t):
        q_plain(t)
        for d in range(2):
            f_send(d, t).wait_recv()
            mine = part_q(1 if d == 0 else X - 1, piece(t), pl.ds(d * half, half))
            fq[d, t] = (mine + fq[d, t].astype(f32)).astype(jnp.bfloat16)
            q_send(d, t, 1).start()

    def mirror(b):
        return remote(sm.at[b], mk.at[b], ms.at[b], mr.at[b], p.sibling())

    def m_start(b):
        sm[b] = part_kv(1 - c, b).astype(jnp.bfloat16)
        mirror(b).start()

    def owner(d, step):
        far = K + 1 - step
        return (z + (far if d == 0 else R - far)) % R

    def k_send(d, step, h):
        src = mk.at[owner(d, step), pl.ds(h * H, H)]
        return remote(src, rk.at[d, step - 1, h], ks.at[d, step - 1, h], kr.at[d, step - 1, h], z_to(d))

    def k_one(d, step, h):
        b = owner(d, step)
        at = pl.ds(h * H, H)
        total = mk[b, at].astype(f32) + part_kv(c, b, at)
        if step > 2 or (step == 2 and h // (PARTS // 2) == d):
            k_send(d, step - 1, h).wait_recv()
            total = total + rk[d, step - 2, h].astype(f32)
        mk[b, at] = total.astype(jnp.bfloat16)
        k_send(d, step, h).start()

    def k_mirrored(step):
        mirror(owner(0, step)).wait_recv()
        if step > 1:
            mirror(owner(1, step)).wait_recv()

    def k_early(step):
        for i in range(PARTS // 2):
            k_one(0, step, PARTS // 2 + i)
            k_one(1, step, i)

    def k_late(step):
        for i in range(PARTS // 2):
            k_one(0, step, i)
            k_one(1, step, PARTS // 2 + i)

    m_start((z + K) % R)
    pl.loop(0, R)(f_start)
    for far in range(K - 1, 0, -1):
        m_start((z + far) % R)
        m_start((z + R - far) % R)
    m_start(z)

    def out_refs(n, head):
        qcol = pl.ds(pl.multiple_of(head * WIDE, WIDE), WIDE)
        kcol = pl.ds(pl.multiple_of(head * HD, HD), HD)
        return (
            (bq.at[n], gq.at[:, qcol]),
            (bk.at[n, 0], gk.at[:, kcol]),
            (bk.at[n, 1], gv.at[:, kcol]),
        )

    def y_send(t, i):
        src, dst = out_refs(piece(t), y)[i]
        return remote(src, dst, ys.at[i, t], yr.at[i, y], p.dev(dy=p.far(R - 1 - t)))

    def y_wait(t, i):
        n = piece(t)
        src, dst = out_refs(n, n)[i]
        remote(src, dst, ys.at[i, t], yr.at[i, n], p.dev(dy=p.far(R - 1 - t))).wait_recv()

    own = [pltpu.make_async_copy(src, dst, loc.at[i]) for i, (src, dst) in enumerate(out_refs(y, y))]

    def q_total(t):
        for d in range(2):
            q_send(d, t, 0).wait_recv()
            q_send(d, t, 1).wait_recv()
        n = piece(t)
        bq[n] = (part_q(0, n) + rq[0, t].astype(f32) + rq[1, t].astype(f32)).astype(jnp.bfloat16)

    def q_home(t):
        q_total(t)
        y_send(t, 0).start()

    def k_out(n, i):
        return remote(out_refs(n, y)[i][0], out_refs(n, y)[i][1], ys.at[i, n], yr.at[i, y], p.at(x, n, z))

    def k_home(h):
        at = pl.ds(h * H, H)
        total = part_kv(c, z, at) + mk[z, at].astype(f32)
        for d in range(2):
            k_send(d, K, h).wait_recv()
            total = total + rk[d, K - 1, h].astype(f32)
        bk[at] = total.astype(jnp.bfloat16)

        @pl.loop(h * H, (h + 1) * H)
        def _(n):
            @pl.when(n != y)
            def _():
                k_out(n, 1).start()
                k_out(n, 2).start()

            @pl.when(n == y)
            def _():
                own[1].start()
                own[2].start()

    k_mirrored(1)
    k_late(1)
    k_mirrored(2)
    k_early(2)
    pl.loop(0, 4)(q_add)
    k_late(2)
    pl.loop(4, R)(q_add)
    k_mirrored(3)
    k_early(3)
    pl.loop(0, 2)(q_home)
    k_late(3)
    pl.loop(2, 4)(q_home)
    k_mirrored(4)
    k_early(4)
    pl.loop(4, 6)(q_home)
    k_late(4)
    pl.loop(6, R - 1)(q_home)
    q_total(R - 1)
    own[0].start()
    mirror(z).wait_recv()
    for h in range(PARTS):
        k_home(h)

    @pl.loop(0, R - 1)
    def _(t):
        for i in range(3):
            y_wait(t, i)

    for copy in own:
        copy.wait()

    @pl.loop(0, R - 1)
    def _(t):
        y_send(t, 0).wait_send()

    @pl.loop(0, R)
    def _(n):
        @pl.when(n != y)
        def _():
            k_out(n, 1).wait_send()
            k_out(n, 2).wait_send()

    @pl.loop(0, R)
    def _(t):
        for d in range(2):
            f_send(d, t).wait_send()
            q_send(d, t, 0).wait_send()
            q_send(d, t, 1).wait_send()
        mirror(t).wait_send()

    for step in range(1, K + 1):
        for h in range(PARTS):
            for d in range(2):
                if step > 1 or h // (PARTS // 2) == d:
                    k_send(d, step, h).wait_send()


def reduce(R, X, dq, dkv):
    K = R // 2
    rows = dq.shape[2]
    anyspace = pl.BlockSpec(memory_space=pl.ANY)
    vmem = pl.BlockSpec(memory_space=pltpu.VMEM)
    dma = pltpu.SemaphoreType.DMA
    bf16 = jnp.bfloat16
    return pl.pallas_call(
        functools.partial(reduce_kernel, R, X),
        out_shape=(
            jax.ShapeDtypeStruct((rows, R * WIDE), bf16),
            jax.ShapeDtypeStruct((rows, R * HD), bf16),
            jax.ShapeDtypeStruct((rows, R * HD), bf16),
        ),
        in_specs=[vmem] * 2,
        out_specs=(anyspace,) * 3,
        scratch_shapes=[
            pltpu.VMEM((2, R, rows // 2, WIDE), bf16),
            pltpu.VMEM((2, R, rows // 2, WIDE), bf16),
            pltpu.VMEM((2, R, rows // 2, WIDE), bf16),
            pltpu.VMEM((2, R, rows, WIDE), bf16),
            pltpu.VMEM(dkv.shape[1:], bf16),
            pltpu.VMEM(dkv.shape[1:], bf16),
            pltpu.VMEM((2, K, PARTS, R // PARTS) + dkv.shape[3:], bf16),
            pltpu.VMEM(dq.shape[1:], bf16),
            pltpu.VMEM(dkv.shape[2:], bf16),
            dma((3, R)),
            dma((3, R)),
            dma((3,)),
            dma((2, R)),
            dma((2, R)),
            dma((2, 2, R)),
            dma((2, 2, R)),
            dma((R,)),
            dma((R,)),
            dma((2, K, PARTS)),
            dma((2, K, PARTS)),
        ],
        compiler_params=pltpu.CompilerParams(
            collective_id=2, has_side_effects=True, vmem_limit_bytes=26 << 20
        ),
        name="reduce_rings",
    )(dq, dkv)


def body(R, X, queries, keys, values, outputs_saved, grad_out, lse, block_lists):
    stats = lse.reshape(2, QB, 2, GROUP).transpose(2, 0, 3, 1).reshape(2, 2 * GROUP, QB)
    lists = lax.dynamic_slice_in_dim(block_lists, 2 * lax.axis_index("seq"), 2, 0)
    lists = lists.reshape(2, 2, GROUP, NSEL).transpose(1, 0, 2, 3).reshape(2, 1, 2 * GROUP * NSEL)
    lists = jnp.pad(lists.astype(jnp.float32), ((0, 0), (0, 7), (0, QB - 2 * GROUP * NSEL)))
    stats = jnp.concatenate([stats, lists], axis=1)
    QD, KV, DL, LS, LI, dq0, dkv0 = gather(
        R, X, queries, grad_out, outputs_saved, keys, values, stats
    )
    dq, dkv = pair_grads(LI, QD, KV, DL, LS, dq0, dkv0)
    return reduce(R, X, dq, dkv)


def solution(mesh):
    R = math.isqrt(mesh.shape["seq"] // 2)
    X = mesh.shape["head"]
    in_specs = (
        P(("seq", "head"), None),
        P(("seq", "head"), None),
        P(("seq", "head"), None),
        P(("seq", "head"), None),
        P(("seq", "head"), None),
        P("seq", "head"),
        P(None, "head", None),
    )
    out_specs = (P(("seq", "head"), None), P(("seq", "head"), None), P(("seq", "head"), None))
    return jax.shard_map(
        functools.partial(body, R, X), mesh=mesh, in_specs=in_specs, out_specs=out_specs, check_vma=False
    )
```

```python
import functools
import math

import jax
import jax.numpy as jnp
from jax import lax
from jax.experimental import pallas as pl
from jax.experimental.pallas import tpu as pltpu
from jax.sharding import PartitionSpec as P

HD = 128
QB = 128
KB = 64
NSEL = 4
GROUP = 4
WIDE = GROUP * HD
MESH = pl.DeviceIdType.MESH
SCALE = HD ** (-0.5)
UNROLL = 4
PARTS = 4


class Place:
    def __init__(self, R, X):
        self.R, self.X = R, X
        self.x = lax.axis_index("head")
        s = lax.axis_index("seq")
        self.c = s % 2
        self.z = (s // 2) % R
        self.y = s // (2 * R)

    def dev(self, dx=0, dy=0, dz=0):
        return self.at((self.x + dx) % self.X, (self.y + dy) % self.R, (self.z + dz) % self.R)

    def at(self, x, y, z):
        return ((y * self.R + z) * 2 + self.c, x)

    def sibling(self):
        return ((self.y * self.R + self.z) * 2 + 1 - self.c, self.x)

    def far(self, t):
        return ((t % 2) * ((t + 1) // 2) + (1 - t % 2) * (self.R - t // 2)) % self.R

    def barrier(self, plane):
        sem = pltpu.get_barrier_semaphore()
        offsets = [(dx, dy) for dx in range(self.X) for dy in range(self.R) if dx or dy]
        near = [(dx, dy) for dx, dy in offsets if not dx or (not dy and dx in (1, self.X - 1))]
        others = [self.dev(dx=dx, dy=dy) for dx, dy in (offsets if plane else near)]
        others += [self.dev(dz=1), self.dev(dz=self.R - 1), self.sibling()]
        for other in others:
            pl.semaphore_signal(sem, inc=1, device_id=other, device_id_type=MESH)
        pl.semaphore_wait(sem, len(others))


def remote(src, dst, s_sem, r_sem, to):
    return pltpu.make_async_remote_copy(
        src_ref=src, dst_ref=dst, send_sem=s_sem, recv_sem=r_sem, device_id=to, device_id_type=MESH
    )


def dot(a, b, ca, cb):
    return lax.dot_general(a, b, (((ca,), (cb,)), ((), ())), preferred_element_type=jnp.float32)


def quot(a, n):
    return lax.shift_right_logical(a, jnp.int32(n.bit_length() - 1))


def rest(a, n):
    return a & jnp.int32(n - 1)


def columns(g):
    return pl.ds(pl.multiple_of(g * HD, HD), HD)


def load_query(QD, DL, LS, n, b, g):
    rows, cols = pl.ds(2 * b, 2), columns(g)
    qv = QD[rows, n, 0, :, cols].reshape(QB, HD)
    dov = QD[rows, n, 1, :, cols].reshape(QB, HD)
    lse = LS[n, pl.ds(b * GROUP + g, 1), :]
    delta = DL[2 * b, n, pl.ds(g, 1), :] + DL[2 * b + 1, n, pl.ds(g, 1), :]
    return qv, dov, lse, delta


def grads(qv, dov, lse, delta, kv, vv, mask=None):
    both = dot(jnp.concatenate([kv, vv], axis=0), jnp.concatenate([qv, dov], axis=0), 1, 1)
    prob = jnp.exp(both[:KB, :QB] * SCALE - lse)
    if mask is not None:
        prob = jnp.where(mask, prob, 0.0)
    ds = (prob * (both[KB:, QB:] - delta)).astype(jnp.bfloat16)
    pb = prob.astype(jnp.bfloat16)
    return dot(ds, kv, 0, 0), dot(ds, qv, 1, 0), dot(pb, dov, 1, 0)


def gather_kernel(
    R, X, q, do, o, k, v, ls, QD, KV, DL, LS, LI, dq0, dkv0, dl, do_v, o_v,
    ys, yr, ls_s, ls_r, loc, qs, qr, fs, fr, ds, dr, ks, kr, ms, mr,
):
    p = Place(R, X)
    K = R // 2
    H = R // 2
    x, y, z, c = p.x, p.y, p.z, p.c
    loads = [
        pltpu.make_async_copy(src, dst, loc.at[6 + i])
        for i, (src, dst) in enumerate(((do, do_v), (o, o_v)))
    ]
    for copy in loads:
        copy.start()
    p.barrier(True)

    def pieces(t):
        head = (y + p.far(t)) % R
        qcol = pl.ds(pl.multiple_of(head * WIDE, WIDE), WIDE)
        kcol = pl.ds(pl.multiple_of(head * HD, HD), HD)
        return (
            (k.at[:, kcol], KV.at[c, z, y, 0]),
            (v.at[:, kcol], KV.at[c, z, y, 1]),
            (q.at[:, qcol], QD.at[x, y, 0]),
            (do.at[:, qcol], QD.at[x, y, 1]),
            (dl.at[head], DL.at[x, y]),
        )

    def y_send(t, i):
        src, dst = pieces(t)[i]
        return remote(src, dst, ys.at[i, t], yr.at[i, y], p.dev(dy=p.far(t)))

    def y_wait(t, i):
        n = (y + p.far(t)) % R
        dst = (KV.at[c, z, n, 0], KV.at[c, z, n, 1], QD.at[x, n, 0], QD.at[x, n, 1], DL.at[x, n])[i]
        remote(dst, dst, ys.at[i, t], yr.at[i, n], p.dev(dy=p.far(t))).wait_recv()

    own = [pltpu.make_async_copy(src, dst, loc.at[i]) for i, (src, dst) in enumerate(pieces(0))]
    for copy in own[:4]:
        copy.start()

    def y_start(t, kinds):
        for i in kinds:
            y_send(t, i).start()

    y_start(1, (2, 3))
    y_start(2, (2, 3))

    @pl.loop(1, R)
    def _(t):
        y_start(t, (0, 1))

    def ls_send(i, dx):
        return remote(
            ls.at[i], LS.at[y], ls_s.at[i, dx], ls_r.at[y], p.at((x + dx) % X, 2 * x + i, z)
        )

    ls_home = y // 2 == x
    ls_own = pltpu.make_async_copy(ls.at[y % 2], LS.at[y], loc.at[5])

    def ls_each(act):
        for i in range(2):
            for dx in range(X):
                if dx:
                    act(ls_send(i, dx))
                else:
                    pl.when(y != 2 * x + i)(functools.partial(act, ls_send(i, dx)))

    ls_each(lambda copy: copy.start())
    pl.when(ls_home)(ls_own.start)

    at_head = lax.broadcasted_iota(jnp.int32, (8, HD), 0)
    picks = [(at_head == g).astype(jnp.bfloat16) for g in range(GROUP)]
    lane = lax.broadcasted_iota(jnp.int32, (8, QB), 1)
    here = (lane // KB) == x % 2

    for copy in loads:
        copy.wait()

    @pl.loop(0, R)
    def _(n):
        cols = pl.ds(pl.multiple_of(n * WIDE, WIDE), WIDE)
        prod = do_v[:, cols].astype(jnp.float32) * o_v[:, cols].astype(jnp.float32)
        high = prod.astype(jnp.bfloat16)
        low = (prod - high.astype(jnp.float32)).astype(jnp.bfloat16)
        tile = jnp.zeros((8, KB), jnp.float32)
        for g in range(GROUP):
            at = slice(g * HD, (g + 1) * HD)
            tile += dot(picks[g], high[:, at], 1, 1) + dot(picks[g], low[:, at], 1, 1)
        dl[n] = jnp.where(here, jnp.concatenate([tile, tile], axis=1), 0.0)

    own[4].start()

    @pl.loop(1, R)
    def _(t):
        y_start(t, (4,))

    @pl.loop(3, R)
    def _(t):
        y_start(t, (2, 3))

    def q_send(d, t):
        n = (y + p.far(t)) % R
        part = QD.at[x, n]
        return remote(part, part, qs.at[d, t], qr.at[d, t], p.dev(dx=1 if d == 0 else X - 1))

    def q_arrived(d, t):
        n = (y + p.far(t)) % R
        part = QD.at[(x + (X - 1 if d == 0 else 1)) % X, n]
        remote(part, part, qs.at[d, t], qr.at[d, t], p.dev(dx=1 if d == 0 else X - 1)).wait_recv()

    def f_send(d, t):
        n = (y + p.far(t)) % R
        part = QD.at[(x + (X - 1 if d == 0 else 1)) % X, n, d]
        return remote(part, part, fs.at[d, t], fr.at[d, t], p.dev(dx=1 if d == 0 else X - 1))

    def f_arrived(d, t):
        n = (y + p.far(t)) % R
        part = QD.at[(x + 2) % X, n, d]
        remote(part, part, fs.at[d, t], fr.at[d, t], p.dev(dx=1 if d == 0 else X - 1)).wait_recv()

    def d_send(d, hop):
        part = DL.at[(x + (0, X - 1 if d == 0 else 1)[hop]) % X]
        return remote(part, part, ds.at[d, hop], dr.at[d, hop], p.dev(dx=1 if d == 0 else X - 1))

    def d_arrived(d, hop):
        part = DL.at[(x + (X - 1 if d == 0 else 1, 2)[hop]) % X]
        remote(part, part, ds.at[d, hop], dr.at[d, hop], p.dev(dx=1 if d == 0 else X - 1)).wait_recv()

    def k_block(d, hops):
        return (z + (R - hops if d == 0 else hops)) % R

    def k_send(d, step, h):
        part = KV.at[c, k_block(d, step - 1), pl.ds(h * H, H)]
        return remote(part, part, ks.at[d, step - 1, h], kr.at[d, step - 1, h], p.dev(dz=1 if d == 0 else R - 1))

    def k_arrived(d, step, h):
        part = KV.at[c, k_block(d, step), pl.ds(h * H, H)]
        remote(
            part, part, ks.at[d, step - 1, h], kr.at[d, step - 1, h], p.dev(dz=1 if d == 0 else R - 1)
        ).wait_recv()

    def mirror(b):
        return remote(KV.at[c, b], KV.at[c, b], ms.at[b], mr.at[b], p.sibling())

    def mirrored(b):
        part = KV.at[1 - c, b]
        remote(part, part, ms.at[b], mr.at[b], p.sibling()).wait_recv()

    def k_first():
        own[0].wait()
        own[1].wait()

        @pl.loop(1, R)
        def _(t):
            y_wait(t, 0)
            y_wait(t, 1)

        for h in range(2):
            k_send(0, 1, h).start()
            k_send(1, 1, h).start()
        mirror(z).start()

    def k_step(step):
        for h in range(2):
            k_arrived(0, step - 1, h)
            if step < K or h == 0:
                k_send(0, step, h).start()
            k_arrived(1, step - 1, h)
            if step < K or h == 1:
                k_send(1, step, h).start()
        mirror(k_block(0, step - 1)).start()
        mirror(k_block(1, step - 1)).start()

    def spread(t):
        for d in range(2):
            q_send(d, t).start()

    def forward(t):
        for d in range(2):
            q_arrived(d, t)
            f_send(d, t).start()

    def d_first():
        own[4].wait()

        @pl.loop(1, R)
        def _(t):
            y_wait(t, 4)

        d_send(0, 0).start()
        d_send(1, 0).start()

    def d_second():
        d_arrived(0, 0)
        d_send(0, 1).start()
        d_arrived(1, 0)

    def stats_arrived():
        @pl.loop(1, R)
        def _(t):
            n = (y + t) % R
            remote(LS.at[n], LS.at[n], ls_s.at[0, 0], ls_r.at[n], p.dev(dy=1)).wait_recv()

        pl.when(ls_home)(ls_own.wait)

        @pl.when(jnp.logical_not(ls_home))
        def _():
            remote(LS.at[y], LS.at[y], ls_s.at[0, 0], ls_r.at[y], p.dev(dy=1)).wait_recv()

        lists = LS[:, 2 * GROUP, :]
        shard = jnp.floor(lists / X)
        chip = jnp.floor(shard / 2)
        ky = jnp.floor(chip / R)
        key = ((shard - 2 * chip) * R + chip - R * ky) * R + ky
        LI[...] = jnp.where(lists - X * shard == x.astype(jnp.float32), key, -1.0).astype(jnp.int32)

    key_at = lax.broadcasted_iota(jnp.int32, (KB, QB), 0) + (x % 2) * KB
    causal = key_at <= lax.broadcasted_iota(jnp.int32, (KB, QB), 1)

    def own_terms(t):
        n = (y + p.far(t)) % R
        kv, vv = KV[c, z, n, 0], KV[c, z, n, 1]
        results = [grads(*load_query(QD, DL, LS, n, x // 2, g), kv, vv, causal) for g in range(GROUP)]
        for g in range(GROUP):
            dq0[:, n, :, g * HD : (g + 1) * HD] = results[g][0].reshape(2, KB, HD)
        dkv0[n, 0] = sum(r[1] for r in results)
        dkv0[n, 1] = sum(r[2] for r in results)

    own[2].wait()
    own[3].wait()
    spread(0)
    for t in range(1, R):
        y_wait(t, 2)
        y_wait(t, 3)
        spread(t)
        if t > 1:
            forward(t - 2)
        if t == 1:
            k_first()
        if t == 2:
            d_first()
            stats_arrived()
        if t == 3:
            d_second()
        if t in (3, 5, 7):
            k_step((t + 1) // 2)
        if t >= 4:
            for e in ((0, 1), (2, 3), (4,), (5,))[t - 4]:
                own_terms(e)

    forward(R - 2)
    forward(R - 1)
    own_terms(R - 2)
    own_terms(R - 1)
    k_arrived(0, K, 0)
    k_arrived(1, K, 1)
    mirror(k_block(0, K)).start()

    @pl.loop(0, R)
    def _(t):
        f_arrived(0, t)
        f_arrived(1, t)

    d_arrived(0, 1)

    @pl.loop(0, R)
    def _(b):
        mirrored(b)

    ls_each(lambda copy: copy.wait_send())

    @pl.loop(1, R)
    def _(t):
        for i in range(5):
            y_send(t, i).wait_send()

    @pl.loop(0, R)
    def _(t):
        for d in range(2):
            q_send(d, t).wait_send()
            f_send(d, t).wait_send()
        mirror(t).wait_send()

    d_send(0, 0).wait_send()
    d_send(1, 0).wait_send()
    d_send(0, 1).wait_send()
    for step in range(1, K + 1):
        for h in range(2):
            if step < K or h == 0:
                k_send(0, step, h).wait_send()
            if step < K or h == 1:
                k_send(1, step, h).wait_send()


def gather(R, X, q, do, o, k, v, ls):
    K = R // 2
    rows = q.shape[0]
    anyspace = pl.BlockSpec(memory_space=pl.ANY)
    vmem = pl.BlockSpec(memory_space=pltpu.VMEM)
    dma = pltpu.SemaphoreType.DMA
    f32 = jnp.float32
    return pl.pallas_call(
        functools.partial(gather_kernel, R, X),
        out_shape=(
            jax.ShapeDtypeStruct((X, R, 2, rows, WIDE), jnp.bfloat16),
            jax.ShapeDtypeStruct((2, R, R, 2, rows, HD), jnp.bfloat16),
            jax.ShapeDtypeStruct((X, R, 8, QB), f32),
            jax.ShapeDtypeStruct((R,) + ls.shape[1:], f32),
            jax.ShapeDtypeStruct((R, QB), jnp.int32),
            jax.ShapeDtypeStruct((2, R, rows, WIDE), f32),
            jax.ShapeDtypeStruct((R, 2, rows, HD), f32),
        ),
        in_specs=[anyspace] * 6,
        out_specs=(vmem,) * 7,
        scratch_shapes=[
            pltpu.VMEM((R, 8, QB), f32),
            pltpu.VMEM(do.shape, do.dtype),
            pltpu.VMEM(o.shape, o.dtype),
            dma((5, R)),
            dma((5, R)),
            dma((2, X)),
            dma((R,)),
            dma((8,)),
            dma((2, R)),
            dma((2, R)),
            dma((2, R)),
            dma((2, R)),
            dma((2, 2)),
            dma((2, 2)),
            dma((2, K, 2)),
            dma((2, K, 2)),
            dma((R,)),
            dma((R,)),
        ],
        compiler_params=pltpu.CompilerParams(
            collective_id=1, has_side_effects=True, vmem_limit_bytes=20 << 20
        ),
        name="gather_rings",
    )(*(pltpu.with_memory_space_constraint(a, pltpu.HBM) for a in (q, do, o, k, v)), ls)


def pair_kernel(LI, QD, KV, DL, LS, dq0, dkv0, dq, dkv, pairs):
    X, R = QD.shape[:2]
    x = lax.axis_index("head")
    s = lax.axis_index("seq")
    c, z = s % 2, (s // 2) % R
    own_b = x // 2
    blocks = 2 * R * R
    listed = GROUP * NSEL

    def scan(i, count):
        dq[i // R, i % R] = jnp.zeros(dq.shape[2:], jnp.float32)
        for e in range(blocks // (X * R)):
            dkv[i * (blocks // (X * R)) + e] = jnp.zeros(dkv.shape[1:], jnp.float32)
        for e in range(2 * R * listed // (X * R)):
            k = i * (2 * R * listed // (X * R)) + e
            key = LI[quot(k, 2 * listed), rest(k, 2 * listed)]
            pairs[count] = quot(k, NSEL) * blocks + key
            count += (key >= 0).astype(jnp.int32)
        return count

    count = lax.fori_loop(0, X * R, scan, jnp.int32(0))
    for e in range(UNROLL):
        pairs[count + e] = 0

    @pl.loop(0, R)
    def _(n):
        dq[pl.ds(2 * own_b, 2), n] = dq0[:, n]
        dkv[(c * R + z) * R + n] = dkv0[n]

    @pl.loop(0, (count + UNROLL - 1) // UNROLL)
    def _(t):
        results = []
        for u in range(UNROLL):
            i = t * UNROLL + u
            code = pairs[i]
            unit, key = quot(code, blocks), rest(code, blocks)
            g, b, n = rest(unit, GROUP), rest(quot(unit, GROUP), 2), quot(unit, 2 * GROUP)
            qv, dov, lse, delta = load_query(QD, DL, LS, n, b, g)
            lse = lse + jnp.where(i < count, 0.0, 1e30)
            results.append((n, b, g, key, grads(qv, dov, lse, delta, KV[key, 0], KV[key, 1])))
        for n, b, g, key, out in results:
            dq[pl.ds(2 * b, 2), n, :, columns(g)] += out[0].reshape(2, KB, HD)
            dkv[key, 0] += out[1]
            dkv[key, 1] += out[2]


def pair_grads(LI, QD, KV, DL, LS, dq0, dkv0):
    vmem = pl.BlockSpec(memory_space=pltpu.VMEM)
    smem = pl.BlockSpec(memory_space=pltpu.SMEM)
    X, R = QD.shape[:2]
    flat = KV.reshape((2 * R * R,) + KV.shape[3:])
    dq, dkv = pl.pallas_call(
        pair_kernel,
        out_shape=(
            jax.ShapeDtypeStruct(QD.shape[:2] + QD.shape[3:], jnp.float32),
            jax.ShapeDtypeStruct(flat.shape, jnp.float32),
        ),
        in_specs=[smem] + [vmem] * 6,
        out_specs=(vmem,) * 2,
        scratch_shapes=[pltpu.SMEM((2 * R * GROUP * NSEL + UNROLL,), jnp.int32)],
        compiler_params=pltpu.CompilerParams(vmem_limit_bytes=28 << 20),
        name="pair_grads",
    )(LI, QD, flat, DL, LS, dq0, dkv0)
    return dq, dkv.reshape(KV.shape)


def reduce_kernel(
    R, X, dq, dkv, gq, gk, gv, sf, sp, fq, rq, sm, mk, rk, bq, bk,
    ys, yr, loc, fs, fr, qs, qr, ms, mr, ks, kr,
):
    p = Place(R, X)
    K = R // 2
    H = R // PARTS
    x, y, z, c = p.x, p.y, p.z, p.c
    rows = dq.shape[2]
    half = rows // 2
    p.barrier(False)
    f32 = jnp.float32

    def piece(t):
        return (y + p.far(R - 1 - t)) % R

    def x_to(d):
        return p.dev(dx=1 if d == 0 else X - 1)

    def z_to(d):
        return p.dev(dz=1 if d == 0 else R - 1)

    def part_q(dx, n, at=slice(None)):
        return dq[(x + dx) % X, n, at] * SCALE

    def part_kv(core, b, at=slice(None)):
        part = dkv[core, b, at]
        return jnp.concatenate([part[:, :1] * SCALE, part[:, 1:]], axis=1)

    def f_send(d, t):
        return remote(sf.at[d, t], fq.at[d, t], fs.at[d, t], fr.at[d, t], x_to(d))

    def f_start(t):
        for d in range(2):
            sf[d, t] = part_q(2, piece(t), pl.ds(d * half, half)).astype(jnp.bfloat16)
            f_send(d, t).start()

    def q_send(d, t, late):
        src = (fq if late else sp).at[d, t]
        dst = rq.at[d, t, pl.ds((d if late else 1 - d) * half, half)]
        return remote(src, dst, qs.at[late, d, t], qr.at[late, d, t], x_to(d))

    def q_plain(t):
        for d in range(2):
            at = pl.ds((1 - d) * half, half)
            sp[d, t] = part_q(1 if d == 0 else X - 1, piece(t), at).astype(jnp.bfloat16)
            q_send(d, t, 0).start()

    def q_add(t):
        q_plain(t)
        for d in range(2):
            f_send(d, t).wait_recv()
            mine = part_q(1 if d == 0 else X - 1, piece(t), pl.ds(d * half, half))
            fq[d, t] = (mine + fq[d, t].astype(f32)).astype(jnp.bfloat16)
            q_send(d, t, 1).start()

    def mirror(b):
        return remote(sm.at[b], mk.at[b], ms.at[b], mr.at[b], p.sibling())

    def m_start(b):
        sm[b] = part_kv(1 - c, b).astype(jnp.bfloat16)
        mirror(b).start()

    def owner(d, step):
        far = K + 1 - step
        return (z + (far if d == 0 else R - far)) % R

    def k_send(d, step, h):
        src = mk.at[owner(d, step), pl.ds(h * H, H)]
        return remote(src, rk.at[d, step - 1, h], ks.at[d, step - 1, h], kr.at[d, step - 1, h], z_to(d))

    def k_one(d, step, h):
        b = owner(d, step)
        at = pl.ds(h * H, H)
        total = mk[b, at].astype(f32) + part_kv(c, b, at)
        if step > 2 or (step == 2 and h // (PARTS // 2) == d):
            k_send(d, step - 1, h).wait_recv()
            total = total + rk[d, step - 2, h].astype(f32)
        mk[b, at] = total.astype(jnp.bfloat16)
        k_send(d, step, h).start()

    def k_mirrored(step):
        mirror(owner(0, step)).wait_recv()
        if step > 1:
            mirror(owner(1, step)).wait_recv()

    def k_early(step):
        for i in range(PARTS // 2):
            k_one(0, step, PARTS // 2 + i)
            k_one(1, step, i)

    def k_late(step):
        for i in range(PARTS // 2):
            k_one(0, step, i)
            k_one(1, step, PARTS // 2 + i)

    m_start((z + K) % R)
    pl.loop(0, R)(f_start)
    for far in range(K - 1, 0, -1):
        m_start((z + far) % R)
        m_start((z + R - far) % R)
    m_start(z)

    def out_refs(n, head):
        qcol = pl.ds(pl.multiple_of(head * WIDE, WIDE), WIDE)
        kcol = pl.ds(pl.multiple_of(head * HD, HD), HD)
        return (
            (bq.at[n], gq.at[:, qcol]),
            (bk.at[n, 0], gk.at[:, kcol]),
            (bk.at[n, 1], gv.at[:, kcol]),
        )

    def y_send(t, i):
        src, dst = out_refs(piece(t), y)[i]
        return remote(src, dst, ys.at[i, t], yr.at[i, y], p.dev(dy=p.far(R - 1 - t)))

    def y_wait(t, i):
        n = piece(t)
        src, dst = out_refs(n, n)[i]
        remote(src, dst, ys.at[i, t], yr.at[i, n], p.dev(dy=p.far(R - 1 - t))).wait_recv()

    own = [pltpu.make_async_copy(src, dst, loc.at[i]) for i, (src, dst) in enumerate(out_refs(y, y))]

    def q_total(t):
        for d in range(2):
            q_send(d, t, 0).wait_recv()
            q_send(d, t, 1).wait_recv()
        n = piece(t)
        bq[n] = (part_q(0, n) + rq[0, t].astype(f32) + rq[1, t].astype(f32)).astype(jnp.bfloat16)

    def q_home(t):
        q_total(t)
        y_send(t, 0).start()

    def k_out(n, i):
        return remote(out_refs(n, y)[i][0], out_refs(n, y)[i][1], ys.at[i, n], yr.at[i, y], p.at(x, n, z))

    def k_home(h):
        at = pl.ds(h * H, H)
        total = part_kv(c, z, at) + mk[z, at].astype(f32)
        for d in range(2):
            k_send(d, K, h).wait_recv()
            total = total + rk[d, K - 1, h].astype(f32)
        bk[at] = total.astype(jnp.bfloat16)

        @pl.loop(h * H, (h + 1) * H)
        def _(n):
            @pl.when(n != y)
            def _():
                k_out(n, 1).start()
                k_out(n, 2).start()

            @pl.when(n == y)
            def _():
                own[1].start()
                own[2].start()

    k_mirrored(1)
    k_late(1)
    k_mirrored(2)
    k_early(2)
    pl.loop(0, 4)(q_add)
    k_late(2)
    pl.loop(4, R)(q_add)
    k_mirrored(3)
    k_early(3)
    pl.loop(0, 2)(q_home)
    k_late(3)
    pl.loop(2, 4)(q_home)
    k_mirrored(4)
    k_early(4)
    pl.loop(4, 6)(q_home)
    k_late(4)
    pl.loop(6, R - 1)(q_home)
    q_total(R - 1)
    own[0].start()
    mirror(z).wait_recv()
    for i in range(PARTS // 2):
        k_home(i)
        k_home(PARTS // 2 + i)

    @pl.loop(0, R - 1)
    def _(t):
        for i in range(3):
            y_wait(t, i)

    for copy in own:
        copy.wait()

    @pl.loop(0, R - 1)
    def _(t):
        y_send(t, 0).wait_send()

    @pl.loop(0, R)
    def _(n):
        @pl.when(n != y)
        def _():
            k_out(n, 1).wait_send()
            k_out(n, 2).wait_send()

    @pl.loop(0, R)
    def _(t):
        for d in range(2):
            f_send(d, t).wait_send()
            q_send(d, t, 0).wait_send()
            q_send(d, t, 1).wait_send()
        mirror(t).wait_send()

    for step in range(1, K + 1):
        for h in range(PARTS):
            for d in range(2):
                if step > 1 or h // (PARTS // 2) == d:
                    k_send(d, step, h).wait_send()


def reduce(R, X, dq, dkv):
    K = R // 2
    rows = dq.shape[2]
    anyspace = pl.BlockSpec(memory_space=pl.ANY)
    vmem = pl.BlockSpec(memory_space=pltpu.VMEM)
    dma = pltpu.SemaphoreType.DMA
    bf16 = jnp.bfloat16
    return pl.pallas_call(
        functools.partial(reduce_kernel, R, X),
        out_shape=(
            jax.ShapeDtypeStruct((rows, R * WIDE), bf16),
            jax.ShapeDtypeStruct((rows, R * HD), bf16),
            jax.ShapeDtypeStruct((rows, R * HD), bf16),
        ),
        in_specs=[vmem] * 2,
        out_specs=(anyspace,) * 3,
        scratch_shapes=[
            pltpu.VMEM((2, R, rows // 2, WIDE), bf16),
            pltpu.VMEM((2, R, rows // 2, WIDE), bf16),
            pltpu.VMEM((2, R, rows // 2, WIDE), bf16),
            pltpu.VMEM((2, R, rows, WIDE), bf16),
            pltpu.VMEM(dkv.shape[1:], bf16),
            pltpu.VMEM(dkv.shape[1:], bf16),
            pltpu.VMEM((2, K, PARTS, R // PARTS) + dkv.shape[3:], bf16),
            pltpu.VMEM(dq.shape[1:], bf16),
            pltpu.VMEM(dkv.shape[2:], bf16),
            dma((3, R)),
            dma((3, R)),
            dma((3,)),
            dma((2, R)),
            dma((2, R)),
            dma((2, 2, R)),
            dma((2, 2, R)),
            dma((R,)),
            dma((R,)),
            dma((2, K, PARTS)),
            dma((2, K, PARTS)),
        ],
        compiler_params=pltpu.CompilerParams(
            collective_id=2, has_side_effects=True, vmem_limit_bytes=26 << 20
        ),
        name="reduce_rings",
    )(dq, dkv)


def finish_kernel(*refs):
    n = len(refs) // 2
    sems = refs[-1]
    copies = [pltpu.make_async_copy(refs[i], refs[n + i], sems.at[i]) for i in range(n)]
    for copy in copies:
        copy.start()
    for copy in copies:
        copy.wait()


def finish(*arrays):
    anyspace = pl.BlockSpec(memory_space=pl.ANY)
    return pl.pallas_call(
        finish_kernel,
        out_shape=tuple(jax.ShapeDtypeStruct(a.shape, a.dtype) for a in arrays),
        in_specs=[anyspace] * len(arrays),
        out_specs=(pl.BlockSpec(memory_space=pltpu.HBM),) * len(arrays),
        scratch_shapes=[pltpu.SemaphoreType.DMA((len(arrays),))],
        name="finish",
    )(*arrays)


def body(R, X, queries, keys, values, outputs_saved, grad_out, lse, block_lists):
    stats = lse.reshape(2, QB, 2, GROUP).transpose(2, 0, 3, 1).reshape(2, 2 * GROUP, QB)
    lists = lax.dynamic_slice_in_dim(block_lists, 2 * lax.axis_index("seq"), 2, 0)
    lists = lists.reshape(2, 2, GROUP, NSEL).transpose(1, 0, 2, 3).reshape(2, 1, 2 * GROUP * NSEL)
    lists = jnp.pad(lists.astype(jnp.float32), ((0, 0), (0, 7), (0, QB - 2 * GROUP * NSEL)))
    stats = jnp.concatenate([stats, lists], axis=1)
    QD, KV, DL, LS, LI, dq0, dkv0 = gather(
        R, X, queries, grad_out, outputs_saved, keys, values, stats
    )
    dq, dkv = pair_grads(LI, QD, KV, DL, LS, dq0, dkv0)
    parts = reduce(R, X, dq, dkv)
    return finish(*(pltpu.with_memory_space_constraint(a, pltpu.VMEM) for a in parts))


def solution(mesh):
    R = math.isqrt(mesh.shape["seq"] // 2)
    X = mesh.shape["head"]
    in_specs = (
        P(("seq", "head"), None),
        P(("seq", "head"), None),
        P(("seq", "head"), None),
        P(("seq", "head"), None),
        P(("seq", "head"), None),
        P("seq", "head"),
        P(None, "head", None),
    )
    out_specs = (P(("seq", "head"), None), P(("seq", "head"), None), P(("seq", "head"), None))
    return jax.shard_map(
        functools.partial(body, R, X), mesh=mesh, in_specs=in_specs, out_specs=out_specs, check_vma=False
    )
```

```python
import functools
import math

import jax
import jax.numpy as jnp
from jax import lax
from jax.experimental import pallas as pl
from jax.experimental.pallas import tpu as pltpu
from jax.sharding import PartitionSpec as P

HD = 128
QB = 128
KB = 64
NSEL = 4
GROUP = 4
WIDE = GROUP * HD
MESH = pl.DeviceIdType.MESH
SCALE = HD ** (-0.5)
UNROLL = 4
PARTS = 4


class Place:
    def __init__(self, R, X):
        self.R, self.X = R, X
        self.x = lax.axis_index("head")
        s = lax.axis_index("seq")
        self.c = s % 2
        self.z = (s // 2) % R
        self.y = s // (2 * R)

    def dev(self, dx=0, dy=0, dz=0):
        return self.at((self.x + dx) % self.X, (self.y + dy) % self.R, (self.z + dz) % self.R)

    def at(self, x, y, z):
        return ((y * self.R + z) * 2 + self.c, x)

    def sibling(self):
        return ((self.y * self.R + self.z) * 2 + 1 - self.c, self.x)

    def far(self, t):
        return ((t % 2) * ((t + 1) // 2) + (1 - t % 2) * (self.R - t // 2)) % self.R

    def barrier(self, plane):
        sem = pltpu.get_barrier_semaphore()
        offsets = [(dx, dy) for dx in range(self.X) for dy in range(self.R) if dx or dy]
        near = [(dx, dy) for dx, dy in offsets if not dx or (not dy and dx in (1, self.X - 1))]
        others = [self.dev(dx=dx, dy=dy) for dx, dy in (offsets if plane else near)]
        others += [self.dev(dz=1), self.dev(dz=self.R - 1), self.sibling()]
        for other in others:
            pl.semaphore_signal(sem, inc=1, device_id=other, device_id_type=MESH)
        pl.semaphore_wait(sem, len(others))


def remote(src, dst, s_sem, r_sem, to):
    return pltpu.make_async_remote_copy(
        src_ref=src, dst_ref=dst, send_sem=s_sem, recv_sem=r_sem, device_id=to, device_id_type=MESH
    )


def dot(a, b, ca, cb):
    return lax.dot_general(a, b, (((ca,), (cb,)), ((), ())), preferred_element_type=jnp.float32)


def quot(a, n):
    return lax.shift_right_logical(a, jnp.int32(n.bit_length() - 1))


def rest(a, n):
    return a & jnp.int32(n - 1)


def columns(g):
    return pl.ds(pl.multiple_of(g * HD, HD), HD)


def load_query(QD, DL, LS, n, b, g):
    rows, cols = pl.ds(2 * b, 2), columns(g)
    qv = QD[rows, n, 0, :, cols].reshape(QB, HD)
    dov = QD[rows, n, 1, :, cols].reshape(QB, HD)
    lse = LS[n, pl.ds(b * GROUP + g, 1), :]
    delta = DL[2 * b, n, pl.ds(g, 1), :] + DL[2 * b + 1, n, pl.ds(g, 1), :]
    return qv, dov, lse, delta


def grads(qv, dov, lse, delta, kv, vv, mask=None):
    both = dot(jnp.concatenate([kv, vv], axis=0), jnp.concatenate([qv, dov], axis=0), 1, 1)
    prob = jnp.exp(both[:KB, :QB] * SCALE - lse)
    if mask is not None:
        prob = jnp.where(mask, prob, 0.0)
    ds = (prob * (both[KB:, QB:] - delta)).astype(jnp.bfloat16)
    pb = prob.astype(jnp.bfloat16)
    return dot(ds, kv, 0, 0), dot(ds, qv, 1, 0), dot(pb, dov, 1, 0)


def gather_kernel(
    R, X, q, do, o, k, v, ls, QD, KV, DL, LS, LI, dq0, dkv0, dl, do_v, o_v,
    ys, yr, ls_s, ls_r, loc, qs, qr, fs, fr, ds, dr, ks, kr, ms, mr,
):
    p = Place(R, X)
    K = R // 2
    H = R // 2
    x, y, z, c = p.x, p.y, p.z, p.c
    loads = [
        pltpu.make_async_copy(src, dst, loc.at[6 + i])
        for i, (src, dst) in enumerate(((do, do_v), (o, o_v)))
    ]
    for copy in loads:
        copy.start()
    p.barrier(True)

    def pieces(t):
        head = (y + p.far(t)) % R
        qcol = pl.ds(pl.multiple_of(head * WIDE, WIDE), WIDE)
        kcol = pl.ds(pl.multiple_of(head * HD, HD), HD)
        return (
            (k.at[:, kcol], KV.at[c, z, y, 0]),
            (v.at[:, kcol], KV.at[c, z, y, 1]),
            (q.at[:, qcol], QD.at[x, y, 0]),
            (do.at[:, qcol], QD.at[x, y, 1]),
            (dl.at[head], DL.at[x, y]),
        )

    def y_send(t, i):
        src, dst = pieces(t)[i]
        return remote(src, dst, ys.at[i, t], yr.at[i, y], p.dev(dy=p.far(t)))

    def y_wait(t, i):
        n = (y + p.far(t)) % R
        dst = (KV.at[c, z, n, 0], KV.at[c, z, n, 1], QD.at[x, n, 0], QD.at[x, n, 1], DL.at[x, n])[i]
        remote(dst, dst, ys.at[i, t], yr.at[i, n], p.dev(dy=p.far(t))).wait_recv()

    own = [pltpu.make_async_copy(src, dst, loc.at[i]) for i, (src, dst) in enumerate(pieces(0))]
    for copy in own[:4]:
        copy.start()

    def y_start(t, kinds):
        for i in kinds:
            y_send(t, i).start()

    y_start(1, (2, 3))
    y_start(2, (2, 3))

    @pl.loop(1, R)
    def _(t):
        y_start(t, (0, 1))

    def ls_send(i, dx):
        return remote(
            ls.at[i], LS.at[y], ls_s.at[i, dx], ls_r.at[y], p.at((x + dx) % X, 2 * x + i, z)
        )

    ls_home = y // 2 == x
    ls_own = pltpu.make_async_copy(ls.at[y % 2], LS.at[y], loc.at[5])

    def ls_each(act):
        for i in range(2):
            for dx in range(X):
                if dx:
                    act(ls_send(i, dx))
                else:
                    pl.when(y != 2 * x + i)(functools.partial(act, ls_send(i, dx)))

    ls_each(lambda copy: copy.start())
    pl.when(ls_home)(ls_own.start)

    at_head = lax.broadcasted_iota(jnp.int32, (8, HD), 0)
    picks = [(at_head == g).astype(jnp.bfloat16) for g in range(GROUP)]
    lane = lax.broadcasted_iota(jnp.int32, (8, QB), 1)
    here = (lane // KB) == x % 2

    for copy in loads:
        copy.wait()

    @pl.loop(0, R)
    def _(n):
        cols = pl.ds(pl.multiple_of(n * WIDE, WIDE), WIDE)
        prod = do_v[:, cols].astype(jnp.float32) * o_v[:, cols].astype(jnp.float32)
        high = prod.astype(jnp.bfloat16)
        low = (prod - high.astype(jnp.float32)).astype(jnp.bfloat16)
        tile = jnp.zeros((8, KB), jnp.float32)
        for g in range(GROUP):
            at = slice(g * HD, (g + 1) * HD)
            tile += dot(picks[g], high[:, at], 1, 1) + dot(picks[g], low[:, at], 1, 1)
        dl[n] = jnp.where(here, jnp.concatenate([tile, tile], axis=1), 0.0)

    own[4].start()

    @pl.loop(1, R)
    def _(t):
        y_start(t, (4,))

    @pl.loop(3, R)
    def _(t):
        y_start(t, (2, 3))

    def q_send(d, t):
        n = (y + p.far(t)) % R
        part = QD.at[x, n]
        return remote(part, part, qs.at[d, t], qr.at[d, t], p.dev(dx=1 if d == 0 else X - 1))

    def q_arrived(d, t):
        n = (y + p.far(t)) % R
        part = QD.at[(x + (X - 1 if d == 0 else 1)) % X, n]
        remote(part, part, qs.at[d, t], qr.at[d, t], p.dev(dx=1 if d == 0 else X - 1)).wait_recv()

    def f_send(d, t):
        n = (y + p.far(t)) % R
        part = QD.at[(x + (X - 1 if d == 0 else 1)) % X, n, d]
        return remote(part, part, fs.at[d, t], fr.at[d, t], p.dev(dx=1 if d == 0 else X - 1))

    def f_arrived(d, t):
        n = (y + p.far(t)) % R
        part = QD.at[(x + 2) % X, n, d]
        remote(part, part, fs.at[d, t], fr.at[d, t], p.dev(dx=1 if d == 0 else X - 1)).wait_recv()

    def d_send(d, hop):
        part = DL.at[(x + (0, X - 1 if d == 0 else 1)[hop]) % X]
        return remote(part, part, ds.at[d, hop], dr.at[d, hop], p.dev(dx=1 if d == 0 else X - 1))

    def d_arrived(d, hop):
        part = DL.at[(x + (X - 1 if d == 0 else 1, 2)[hop]) % X]
        remote(part, part, ds.at[d, hop], dr.at[d, hop], p.dev(dx=1 if d == 0 else X - 1)).wait_recv()

    def k_block(d, hops):
        return (z + (R - hops if d == 0 else hops)) % R

    def k_send(d, step, h):
        part = KV.at[c, k_block(d, step - 1), pl.ds(h * H, H)]
        return remote(part, part, ks.at[d, step - 1, h], kr.at[d, step - 1, h], p.dev(dz=1 if d == 0 else R - 1))

    def k_arrived(d, step, h):
        part = KV.at[c, k_block(d, step), pl.ds(h * H, H)]
        remote(
            part, part, ks.at[d, step - 1, h], kr.at[d, step - 1, h], p.dev(dz=1 if d == 0 else R - 1)
        ).wait_recv()

    def mirror(b):
        return remote(KV.at[c, b], KV.at[c, b], ms.at[b], mr.at[b], p.sibling())

    def mirrored(b):
        part = KV.at[1 - c, b]
        remote(part, part, ms.at[b], mr.at[b], p.sibling()).wait_recv()

    def k_first():
        own[0].wait()
        own[1].wait()

        @pl.loop(1, R)
        def _(t):
            y_wait(t, 0)
            y_wait(t, 1)

        for h in range(2):
            k_send(0, 1, h).start()
            k_send(1, 1, h).start()
        mirror(z).start()

    def k_step(step):
        for h in range(2):
            k_arrived(0, step - 1, h)
            if step < K or h == 0:
                k_send(0, step, h).start()
            k_arrived(1, step - 1, h)
            if step < K or h == 1:
                k_send(1, step, h).start()
        mirror(k_block(0, step - 1)).start()
        mirror(k_block(1, step - 1)).start()

    def spread(t):
        for d in range(2):
            q_send(d, t).start()

    def forward(t):
        for d in range(2):
            q_arrived(d, t)
            f_send(d, t).start()

    def d_first():
        own[4].wait()

        @pl.loop(1, R)
        def _(t):
            y_wait(t, 4)

        d_send(0, 0).start()
        d_send(1, 0).start()

    def d_second():
        d_arrived(0, 0)
        d_send(0, 1).start()
        d_arrived(1, 0)

    def stats_arrived():
        @pl.loop(1, R)
        def _(t):
            n = (y + t) % R
            remote(LS.at[n], LS.at[n], ls_s.at[0, 0], ls_r.at[n], p.dev(dy=1)).wait_recv()

        pl.when(ls_home)(ls_own.wait)

        @pl.when(jnp.logical_not(ls_home))
        def _():
            remote(LS.at[y], LS.at[y], ls_s.at[0, 0], ls_r.at[y], p.dev(dy=1)).wait_recv()

        lists = LS[:, 2 * GROUP, :]
        shard = jnp.floor(lists / X)
        chip = jnp.floor(shard / 2)
        ky = jnp.floor(chip / R)
        key = ((shard - 2 * chip) * R + chip - R * ky) * R + ky
        LI[...] = jnp.where(lists - X * shard == x.astype(jnp.float32), key, -1.0).astype(jnp.int32)

    key_at = lax.broadcasted_iota(jnp.int32, (KB, QB), 0) + (x % 2) * KB
    causal = key_at <= lax.broadcasted_iota(jnp.int32, (KB, QB), 1)

    def own_terms(t):
        n = (y + p.far(t)) % R
        kv, vv = KV[c, z, n, 0], KV[c, z, n, 1]
        results = [grads(*load_query(QD, DL, LS, n, x // 2, g), kv, vv, causal) for g in range(GROUP)]
        for g in range(GROUP):
            dq0[:, n, :, g * HD : (g + 1) * HD] = results[g][0].reshape(2, KB, HD)
        dkv0[n, 0] = sum(r[1] for r in results)
        dkv0[n, 1] = sum(r[2] for r in results)

    own[2].wait()
    own[3].wait()
    spread(0)
    for t in range(1, R):
        y_wait(t, 2)
        y_wait(t, 3)
        spread(t)
        if t > 1:
            forward(t - 2)
        if t == 1:
            k_first()
        if t == 2:
            d_first()
            stats_arrived()
        if t == 3:
            d_second()
        if t in (3, 5, 7):
            k_step((t + 1) // 2)
        if t >= 4:
            for e in ((0, 1), (2, 3), (4,), (5,))[t - 4]:
                own_terms(e)

    forward(R - 2)
    k_arrived(0, K, 0)
    k_arrived(1, K, 1)
    mirror(k_block(0, K)).start()
    own_terms(R - 2)
    forward(R - 1)
    own_terms(R - 1)
    @pl.loop(0, R)
    def _(t):
        f_arrived(0, t)
        f_arrived(1, t)

    d_arrived(0, 1)

    @pl.loop(0, R)
    def _(b):
        mirrored(b)

    ls_each(lambda copy: copy.wait_send())

    @pl.loop(1, R)
    def _(t):
        for i in range(5):
            y_send(t, i).wait_send()

    @pl.loop(0, R)
    def _(t):
        for d in range(2):
            q_send(d, t).wait_send()
            f_send(d, t).wait_send()
        mirror(t).wait_send()

    d_send(0, 0).wait_send()
    d_send(1, 0).wait_send()
    d_send(0, 1).wait_send()
    for step in range(1, K + 1):
        for h in range(2):
            if step < K or h == 0:
                k_send(0, step, h).wait_send()
            if step < K or h == 1:
                k_send(1, step, h).wait_send()


def gather(R, X, q, do, o, k, v, ls):
    K = R // 2
    rows = q.shape[0]
    anyspace = pl.BlockSpec(memory_space=pl.ANY)
    vmem = pl.BlockSpec(memory_space=pltpu.VMEM)
    dma = pltpu.SemaphoreType.DMA
    f32 = jnp.float32
    return pl.pallas_call(
        functools.partial(gather_kernel, R, X),
        out_shape=(
            jax.ShapeDtypeStruct((X, R, 2, rows, WIDE), jnp.bfloat16),
            jax.ShapeDtypeStruct((2, R, R, 2, rows, HD), jnp.bfloat16),
            jax.ShapeDtypeStruct((X, R, 8, QB), f32),
            jax.ShapeDtypeStruct((R,) + ls.shape[1:], f32),
            jax.ShapeDtypeStruct((R, QB), jnp.int32),
            jax.ShapeDtypeStruct((2, R, rows, WIDE), f32),
            jax.ShapeDtypeStruct((R, 2, rows, HD), f32),
        ),
        in_specs=[anyspace] * 6,
        out_specs=(vmem,) * 7,
        scratch_shapes=[
            pltpu.VMEM((R, 8, QB), f32),
            pltpu.VMEM(do.shape, do.dtype),
            pltpu.VMEM(o.shape, o.dtype),
            dma((5, R)),
            dma((5, R)),
            dma((2, X)),
            dma((R,)),
            dma((8,)),
            dma((2, R)),
            dma((2, R)),
            dma((2, R)),
            dma((2, R)),
            dma((2, 2)),
            dma((2, 2)),
            dma((2, K, 2)),
            dma((2, K, 2)),
            dma((R,)),
            dma((R,)),
        ],
        compiler_params=pltpu.CompilerParams(
            collective_id=1, has_side_effects=True, vmem_limit_bytes=20 << 20
        ),
        name="gather_rings",
    )(*(pltpu.with_memory_space_constraint(a, pltpu.HBM) for a in (q, do, o, k, v)), ls)


def pair_kernel(LI, QD, KV, DL, LS, dq0, dkv0, dq, dkv, pairs):
    X, R = QD.shape[:2]
    x = lax.axis_index("head")
    s = lax.axis_index("seq")
    c, z = s % 2, (s // 2) % R
    own_b = x // 2
    blocks = 2 * R * R
    listed = GROUP * NSEL

    def scan(i, count):
        dq[i // R, i % R] = jnp.zeros(dq.shape[2:], jnp.float32)
        for e in range(blocks // (X * R)):
            dkv[i * (blocks // (X * R)) + e] = jnp.zeros(dkv.shape[1:], jnp.float32)
        for e in range(2 * R * listed // (X * R)):
            k = i * (2 * R * listed // (X * R)) + e
            key = LI[quot(k, 2 * listed), rest(k, 2 * listed)]
            pairs[count] = quot(k, NSEL) * blocks + key
            count += (key >= 0).astype(jnp.int32)
        return count

    count = lax.fori_loop(0, X * R, scan, jnp.int32(0))
    for e in range(UNROLL):
        pairs[count + e] = 0

    @pl.loop(0, R)
    def _(n):
        dq[pl.ds(2 * own_b, 2), n] = dq0[:, n]
        dkv[(c * R + z) * R + n] = dkv0[n]

    @pl.loop(0, (count + UNROLL - 1) // UNROLL)
    def _(t):
        results = []
        for u in range(UNROLL):
            i = t * UNROLL + u
            code = pairs[i]
            unit, key = quot(code, blocks), rest(code, blocks)
            g, b, n = rest(unit, GROUP), rest(quot(unit, GROUP), 2), quot(unit, 2 * GROUP)
            qv, dov, lse, delta = load_query(QD, DL, LS, n, b, g)
            lse = lse + jnp.where(i < count, 0.0, 1e30)
            results.append((n, b, g, key, grads(qv, dov, lse, delta, KV[key, 0], KV[key, 1])))
        for n, b, g, key, out in results:
            dq[pl.ds(2 * b, 2), n, :, columns(g)] += out[0].reshape(2, KB, HD)
            dkv[key, 0] += out[1]
            dkv[key, 1] += out[2]


def pair_grads(LI, QD, KV, DL, LS, dq0, dkv0):
    vmem = pl.BlockSpec(memory_space=pltpu.VMEM)
    smem = pl.BlockSpec(memory_space=pltpu.SMEM)
    X, R = QD.shape[:2]
    flat = KV.reshape((2 * R * R,) + KV.shape[3:])
    dq, dkv = pl.pallas_call(
        pair_kernel,
        out_shape=(
            jax.ShapeDtypeStruct(QD.shape[:2] + QD.shape[3:], jnp.float32),
            jax.ShapeDtypeStruct(flat.shape, jnp.float32),
        ),
        in_specs=[smem] + [vmem] * 6,
        out_specs=(vmem,) * 2,
        scratch_shapes=[pltpu.SMEM((2 * R * GROUP * NSEL + UNROLL,), jnp.int32)],
        compiler_params=pltpu.CompilerParams(vmem_limit_bytes=28 << 20),
        name="pair_grads",
    )(LI, QD, flat, DL, LS, dq0, dkv0)
    return dq, dkv.reshape(KV.shape)


def reduce_kernel(
    R, X, dq, dkv, gq, gk, gv, sf, sp, fq, rq, sm, mk, rk, bq, bk,
    ys, yr, loc, fs, fr, qs, qr, ms, mr, ks, kr,
):
    p = Place(R, X)
    K = R // 2
    H = R // PARTS
    x, y, z, c = p.x, p.y, p.z, p.c
    rows = dq.shape[2]
    half = rows // 2
    p.barrier(False)
    f32 = jnp.float32

    def piece(t):
        return (y + p.far(R - 1 - t)) % R

    def x_to(d):
        return p.dev(dx=1 if d == 0 else X - 1)

    def z_to(d):
        return p.dev(dz=1 if d == 0 else R - 1)

    def part_q(dx, n, at=slice(None)):
        return dq[(x + dx) % X, n, at] * SCALE

    def part_kv(core, b, at=slice(None)):
        part = dkv[core, b, at]
        return jnp.concatenate([part[:, :1] * SCALE, part[:, 1:]], axis=1)

    def f_send(d, t):
        return remote(sf.at[d, t], fq.at[d, t], fs.at[d, t], fr.at[d, t], x_to(d))

    def f_start(t):
        for d in range(2):
            sf[d, t] = part_q(2, piece(t), pl.ds(d * half, half)).astype(jnp.bfloat16)
            f_send(d, t).start()

    def q_send(d, t, late):
        src = (fq if late else sp).at[d, t]
        dst = rq.at[d, t, pl.ds((d if late else 1 - d) * half, half)]
        return remote(src, dst, qs.at[late, d, t], qr.at[late, d, t], x_to(d))

    def q_plain(t):
        for d in range(2):
            at = pl.ds((1 - d) * half, half)
            sp[d, t] = part_q(1 if d == 0 else X - 1, piece(t), at).astype(jnp.bfloat16)
            q_send(d, t, 0).start()

    def q_add(t):
        q_plain(t)
        for d in range(2):
            f_send(d, t).wait_recv()
            mine = part_q(1 if d == 0 else X - 1, piece(t), pl.ds(d * half, half))
            fq[d, t] = (mine + fq[d, t].astype(f32)).astype(jnp.bfloat16)
            q_send(d, t, 1).start()

    def mirror(b):
        return remote(sm.at[b], mk.at[b], ms.at[b], mr.at[b], p.sibling())

    def m_start(b):
        sm[b] = part_kv(1 - c, b).astype(jnp.bfloat16)
        mirror(b).start()

    def owner(d, step):
        far = K + 1 - step
        return (z + (far if d == 0 else R - far)) % R

    def k_send(d, step, h):
        src = mk.at[owner(d, step), pl.ds(h * H, H)]
        return remote(src, rk.at[d, step - 1, h], ks.at[d, step - 1, h], kr.at[d, step - 1, h], z_to(d))

    def k_one(d, step, h):
        b = owner(d, step)
        at = pl.ds(h * H, H)
        total = mk[b, at].astype(f32) + part_kv(c, b, at)
        if step > 2 or (step == 2 and h // (PARTS // 2) == d):
            k_send(d, step - 1, h).wait_recv()
            total = total + rk[d, step - 2, h].astype(f32)
        mk[b, at] = total.astype(jnp.bfloat16)
        k_send(d, step, h).start()

    def k_mirrored(step):
        mirror(owner(0, step)).wait_recv()
        if step > 1:
            mirror(owner(1, step)).wait_recv()

    def k_early(step):
        for i in range(PARTS // 2):
            k_one(0, step, PARTS // 2 + i)
            k_one(1, step, i)

    def k_late(step):
        for i in range(PARTS // 2):
            k_one(0, step, i)
            k_one(1, step, PARTS // 2 + i)

    m_start((z + K) % R)
    pl.loop(0, R)(f_start)
    for far in range(K - 1, 0, -1):
        m_start((z + far) % R)
        m_start((z + R - far) % R)
    m_start(z)

    def out_refs(n, head):
        qcol = pl.ds(pl.multiple_of(head * WIDE, WIDE), WIDE)
        kcol = pl.ds(pl.multiple_of(head * HD, HD), HD)
        return (
            (bq.at[n], gq.at[:, qcol]),
            (bk.at[n, 0], gk.at[:, kcol]),
            (bk.at[n, 1], gv.at[:, kcol]),
        )

    def y_send(t, i):
        src, dst = out_refs(piece(t), y)[i]
        return remote(src, dst, ys.at[i, t], yr.at[i, y], p.dev(dy=p.far(R - 1 - t)))

    def y_wait(t, i):
        n = piece(t)
        src, dst = out_refs(n, n)[i]
        remote(src, dst, ys.at[i, t], yr.at[i, n], p.dev(dy=p.far(R - 1 - t))).wait_recv()

    own = [pltpu.make_async_copy(src, dst, loc.at[i]) for i, (src, dst) in enumerate(out_refs(y, y))]

    def q_total(t):
        for d in range(2):
            q_send(d, t, 0).wait_recv()
            q_send(d, t, 1).wait_recv()
        n = piece(t)
        bq[n] = (part_q(0, n) + rq[0, t].astype(f32) + rq[1, t].astype(f32)).astype(jnp.bfloat16)

    def q_home(t):
        q_total(t)
        y_send(t, 0).start()

    def k_out(n, i):
        return remote(out_refs(n, y)[i][0], out_refs(n, y)[i][1], ys.at[i, n], yr.at[i, y], p.at(x, n, z))

    def k_home(h):
        at = pl.ds(h * H, H)
        total = part_kv(c, z, at) + mk[z, at].astype(f32)
        for d in range(2):
            k_send(d, K, h).wait_recv()
            total = total + rk[d, K - 1, h].astype(f32)
        bk[at] = total.astype(jnp.bfloat16)

        @pl.loop(h * H, (h + 1) * H)
        def _(n):
            @pl.when(n != y)
            def _():
                k_out(n, 1).start()
                k_out(n, 2).start()

            @pl.when(n == y)
            def _():
                own[1].start()
                own[2].start()

    k_mirrored(1)
    k_late(1)
    k_mirrored(2)
    k_early(2)
    pl.loop(0, 4)(q_add)
    k_late(2)
    pl.loop(4, R)(q_add)
    k_mirrored(3)
    k_early(3)
    pl.loop(0, 2)(q_home)
    k_late(3)
    pl.loop(2, 4)(q_home)
    k_mirrored(4)
    k_early(4)
    pl.loop(4, 6)(q_home)
    k_late(4)
    pl.loop(6, R - 1)(q_home)
    q_total(R - 1)
    own[0].start()
    mirror(z).wait_recv()
    for i in range(PARTS // 2):
        k_home(i)
        k_home(PARTS // 2 + i)

    @pl.loop(0, R - 1)
    def _(t):
        for i in range(3):
            y_wait(t, i)

    for copy in own:
        copy.wait()

    @pl.loop(0, R - 1)
    def _(t):
        y_send(t, 0).wait_send()

    @pl.loop(0, R)
    def _(n):
        @pl.when(n != y)
        def _():
            k_out(n, 1).wait_send()
            k_out(n, 2).wait_send()

    @pl.loop(0, R)
    def _(t):
        for d in range(2):
            f_send(d, t).wait_send()
            q_send(d, t, 0).wait_send()
            q_send(d, t, 1).wait_send()
        mirror(t).wait_send()

    for step in range(1, K + 1):
        for h in range(PARTS):
            for d in range(2):
                if step > 1 or h // (PARTS // 2) == d:
                    k_send(d, step, h).wait_send()


def reduce(R, X, dq, dkv):
    K = R // 2
    rows = dq.shape[2]
    anyspace = pl.BlockSpec(memory_space=pl.ANY)
    vmem = pl.BlockSpec(memory_space=pltpu.VMEM)
    dma = pltpu.SemaphoreType.DMA
    bf16 = jnp.bfloat16
    return pl.pallas_call(
        functools.partial(reduce_kernel, R, X),
        out_shape=(
            jax.ShapeDtypeStruct((rows, R * WIDE), bf16),
            jax.ShapeDtypeStruct((rows, R * HD), bf16),
            jax.ShapeDtypeStruct((rows, R * HD), bf16),
        ),
        in_specs=[vmem] * 2,
        out_specs=(anyspace,) * 3,
        scratch_shapes=[
            pltpu.VMEM((2, R, rows // 2, WIDE), bf16),
            pltpu.VMEM((2, R, rows // 2, WIDE), bf16),
            pltpu.VMEM((2, R, rows // 2, WIDE), bf16),
            pltpu.VMEM((2, R, rows, WIDE), bf16),
            pltpu.VMEM(dkv.shape[1:], bf16),
            pltpu.VMEM(dkv.shape[1:], bf16),
            pltpu.VMEM((2, K, PARTS, R // PARTS) + dkv.shape[3:], bf16),
            pltpu.VMEM(dq.shape[1:], bf16),
            pltpu.VMEM(dkv.shape[2:], bf16),
            dma((3, R)),
            dma((3, R)),
            dma((3,)),
            dma((2, R)),
            dma((2, R)),
            dma((2, 2, R)),
            dma((2, 2, R)),
            dma((R,)),
            dma((R,)),
            dma((2, K, PARTS)),
            dma((2, K, PARTS)),
        ],
        compiler_params=pltpu.CompilerParams(
            collective_id=2, has_side_effects=True, vmem_limit_bytes=26 << 20
        ),
        name="reduce_rings",
    )(dq, dkv)


def finish_kernel(*refs):
    n = len(refs) // 2
    sems = refs[-1]
    copies = [pltpu.make_async_copy(refs[i], refs[n + i], sems.at[i]) for i in range(n)]
    for copy in copies:
        copy.start()
    for copy in copies:
        copy.wait()


def finish(*arrays):
    anyspace = pl.BlockSpec(memory_space=pl.ANY)
    return pl.pallas_call(
        finish_kernel,
        out_shape=tuple(jax.ShapeDtypeStruct(a.shape, a.dtype) for a in arrays),
        in_specs=[anyspace] * len(arrays),
        out_specs=(pl.BlockSpec(memory_space=pltpu.HBM),) * len(arrays),
        scratch_shapes=[pltpu.SemaphoreType.DMA((len(arrays),))],
        name="finish",
    )(*arrays)


def body(R, X, queries, keys, values, outputs_saved, grad_out, lse, block_lists):
    stats = lse.reshape(2, QB, 2, GROUP).transpose(2, 0, 3, 1).reshape(2, 2 * GROUP, QB)
    lists = lax.dynamic_slice_in_dim(block_lists, 2 * lax.axis_index("seq"), 2, 0)
    lists = lists.reshape(2, 2, GROUP, NSEL).transpose(1, 0, 2, 3).reshape(2, 1, 2 * GROUP * NSEL)
    lists = jnp.pad(lists.astype(jnp.float32), ((0, 0), (0, 7), (0, QB - 2 * GROUP * NSEL)))
    stats = jnp.concatenate([stats, lists], axis=1)
    QD, KV, DL, LS, LI, dq0, dkv0 = gather(
        R, X, queries, grad_out, outputs_saved, keys, values, stats
    )
    dq, dkv = pair_grads(LI, QD, KV, DL, LS, dq0, dkv0)
    parts = reduce(R, X, dq, dkv)
    return finish(*(pltpu.with_memory_space_constraint(a, pltpu.VMEM) for a in parts))


def solution(mesh):
    R = math.isqrt(mesh.shape["seq"] // 2)
    X = mesh.shape["head"]
    in_specs = (
        P(("seq", "head"), None),
        P(("seq", "head"), None),
        P(("seq", "head"), None),
        P(("seq", "head"), None),
        P(("seq", "head"), None),
        P("seq", "head"),
        P(None, "head", None),
    )
    out_specs = (P(("seq", "head"), None), P(("seq", "head"), None), P(("seq", "head"), None))
    return jax.shard_map(
        functools.partial(body, R, X), mesh=mesh, in_specs=in_specs, out_specs=out_specs, check_vma=False
    )
```

```python
import functools
import math

import jax
import jax.numpy as jnp
from jax import lax
from jax.experimental import pallas as pl
from jax.experimental.pallas import tpu as pltpu
from jax.sharding import PartitionSpec as P

HD = 128
QB = 128
KB = 64
NSEL = 4
GROUP = 4
WIDE = GROUP * HD
MESH = pl.DeviceIdType.MESH
SCALE = HD ** (-0.5)
UNROLL = 4
PARTS = 4


class Place:
    def __init__(self, R, X):
        self.R, self.X = R, X
        self.x = lax.axis_index("head")
        s = lax.axis_index("seq")
        self.c = s % 2
        self.z = (s // 2) % R
        self.y = s // (2 * R)

    def dev(self, dx=0, dy=0, dz=0):
        return self.at((self.x + dx) % self.X, (self.y + dy) % self.R, (self.z + dz) % self.R)

    def at(self, x, y, z):
        return ((y * self.R + z) * 2 + self.c, x)

    def sibling(self):
        return ((self.y * self.R + self.z) * 2 + 1 - self.c, self.x)

    def far(self, t):
        return ((t % 2) * ((t + 1) // 2) + (1 - t % 2) * (self.R - t // 2)) % self.R

    def barrier(self, plane):
        sem = pltpu.get_barrier_semaphore()
        offsets = [(dx, dy) for dx in range(self.X) for dy in range(self.R) if dx or dy]
        near = [(dx, dy) for dx, dy in offsets if not dx or (not dy and dx in (1, self.X - 1))]
        others = [self.dev(dx=dx, dy=dy) for dx, dy in (offsets if plane else near)]
        others += [self.dev(dz=1), self.dev(dz=self.R - 1), self.sibling()]
        for other in others:
            pl.semaphore_signal(sem, inc=1, device_id=other, device_id_type=MESH)
        pl.semaphore_wait(sem, len(others))


def remote(src, dst, s_sem, r_sem, to):
    return pltpu.make_async_remote_copy(
        src_ref=src, dst_ref=dst, send_sem=s_sem, recv_sem=r_sem, device_id=to, device_id_type=MESH
    )


def dot(a, b, ca, cb):
    return lax.dot_general(a, b, (((ca,), (cb,)), ((), ())), preferred_element_type=jnp.float32)


def quot(a, n):
    return lax.shift_right_logical(a, jnp.int32(n.bit_length() - 1))


def rest(a, n):
    return a & jnp.int32(n - 1)


def columns(g):
    return pl.ds(pl.multiple_of(g * HD, HD), HD)


def load_query(QD, DL, LS, n, b, g):
    rows, cols = pl.ds(2 * b, 2), columns(g)
    qv = QD[rows, n, 0, :, cols].reshape(QB, HD)
    dov = QD[rows, n, 1, :, cols].reshape(QB, HD)
    lse = LS[n, pl.ds(b * GROUP + g, 1), :]
    delta = DL[2 * b, n, pl.ds(g, 1), :] + DL[2 * b + 1, n, pl.ds(g, 1), :]
    return qv, dov, lse, delta


def grads(qv, dov, lse, delta, kv, vv, mask=None):
    both = dot(jnp.concatenate([kv, vv], axis=0), jnp.concatenate([qv, dov], axis=0), 1, 1)
    prob = jnp.exp(both[:KB, :QB] * SCALE - lse)
    if mask is not None:
        prob = jnp.where(mask, prob, 0.0)
    ds = (prob * (both[KB:, QB:] - delta)).astype(jnp.bfloat16)
    pb = prob.astype(jnp.bfloat16)
    return dot(ds, kv, 0, 0), dot(ds, qv, 1, 0), dot(pb, dov, 1, 0)


def gather_kernel(
    R, X, q, do, o, k, v, ls, QD, KV, DL, LS, LI, dq0, dkv0, dl, do_v, o_v,
    ys, yr, ls_s, ls_r, loc, qs, qr, fs, fr, ds, dr, ks, kr, ms, mr,
):
    p = Place(R, X)
    K = R // 2
    H = R // 2
    x, y, z, c = p.x, p.y, p.z, p.c
    loads = [
        pltpu.make_async_copy(src, dst, loc.at[6 + i])
        for i, (src, dst) in enumerate(((do, do_v), (o, o_v)))
    ]
    for copy in loads:
        copy.start()
    p.barrier(True)

    def pieces(t):
        head = (y + p.far(t)) % R
        qcol = pl.ds(pl.multiple_of(head * WIDE, WIDE), WIDE)
        kcol = pl.ds(pl.multiple_of(head * HD, HD), HD)
        return (
            (k.at[:, kcol], KV.at[c, z, y, 0]),
            (v.at[:, kcol], KV.at[c, z, y, 1]),
            (q.at[:, qcol], QD.at[x, y, 0]),
            (do.at[:, qcol], QD.at[x, y, 1]),
            (dl.at[head], DL.at[x, y]),
        )

    def y_send(t, i):
        src, dst = pieces(t)[i]
        return remote(src, dst, ys.at[i, t], yr.at[i, y], p.dev(dy=p.far(t)))

    def y_wait(t, i):
        n = (y + p.far(t)) % R
        dst = (KV.at[c, z, n, 0], KV.at[c, z, n, 1], QD.at[x, n, 0], QD.at[x, n, 1], DL.at[x, n])[i]
        remote(dst, dst, ys.at[i, t], yr.at[i, n], p.dev(dy=p.far(t))).wait_recv()

    own = [pltpu.make_async_copy(src, dst, loc.at[i]) for i, (src, dst) in enumerate(pieces(0))]
    for copy in own[:4]:
        copy.start()

    def y_start(t, kinds):
        for i in kinds:
            y_send(t, i).start()

    y_start(1, (2, 3))
    y_start(2, (2, 3))

    @pl.loop(1, R)
    def _(t):
        y_start(t, (0, 1))

    def ls_send(i, dx):
        return remote(
            ls.at[i], LS.at[y], ls_s.at[i, dx], ls_r.at[y], p.at((x + dx) % X, 2 * x + i, z)
        )

    ls_home = y // 2 == x
    ls_own = pltpu.make_async_copy(ls.at[y % 2], LS.at[y], loc.at[5])

    def ls_each(act):
        for i in range(2):
            for dx in range(X):
                if dx:
                    act(ls_send(i, dx))
                else:
                    pl.when(y != 2 * x + i)(functools.partial(act, ls_send(i, dx)))

    ls_each(lambda copy: copy.start())
    pl.when(ls_home)(ls_own.start)

    at_head = lax.broadcasted_iota(jnp.int32, (8, HD), 0)
    picks = [(at_head == g).astype(jnp.bfloat16) for g in range(GROUP)]
    lane = lax.broadcasted_iota(jnp.int32, (8, QB), 1)
    here = (lane // KB) == x % 2

    for copy in loads:
        copy.wait()

    @pl.loop(0, R)
    def _(n):
        cols = pl.ds(pl.multiple_of(n * WIDE, WIDE), WIDE)
        prod = do_v[:, cols].astype(jnp.float32) * o_v[:, cols].astype(jnp.float32)
        high = prod.astype(jnp.bfloat16)
        low = (prod - high.astype(jnp.float32)).astype(jnp.bfloat16)
        tile = jnp.zeros((8, KB), jnp.float32)
        for g in range(GROUP):
            at = slice(g * HD, (g + 1) * HD)
            tile += dot(picks[g], high[:, at], 1, 1) + dot(picks[g], low[:, at], 1, 1)
        dl[n] = jnp.where(here, jnp.concatenate([tile, tile], axis=1), 0.0)

    own[4].start()

    @pl.loop(1, R)
    def _(t):
        y_start(t, (4,))

    @pl.loop(3, R)
    def _(t):
        y_start(t, (2, 3))

    def q_send(d, t):
        n = (y + p.far(t)) % R
        part = QD.at[x, n]
        return remote(part, part, qs.at[d, t], qr.at[d, t], p.dev(dx=1 if d == 0 else X - 1))

    def q_arrived(d, t):
        n = (y + p.far(t)) % R
        part = QD.at[(x + (X - 1 if d == 0 else 1)) % X, n]
        remote(part, part, qs.at[d, t], qr.at[d, t], p.dev(dx=1 if d == 0 else X - 1)).wait_recv()

    def f_send(d, t):
        n = (y + p.far(t)) % R
        part = QD.at[(x + (X - 1 if d == 0 else 1)) % X, n, d]
        return remote(part, part, fs.at[d, t], fr.at[d, t], p.dev(dx=1 if d == 0 else X - 1))

    def f_arrived(d, t):
        n = (y + p.far(t)) % R
        part = QD.at[(x + 2) % X, n, d]
        remote(part, part, fs.at[d, t], fr.at[d, t], p.dev(dx=1 if d == 0 else X - 1)).wait_recv()

    def d_send(d, hop):
        part = DL.at[(x + (0, X - 1 if d == 0 else 1)[hop]) % X]
        return remote(part, part, ds.at[d, hop], dr.at[d, hop], p.dev(dx=1 if d == 0 else X - 1))

    def d_arrived(d, hop):
        part = DL.at[(x + (X - 1 if d == 0 else 1, 2)[hop]) % X]
        remote(part, part, ds.at[d, hop], dr.at[d, hop], p.dev(dx=1 if d == 0 else X - 1)).wait_recv()

    def k_block(d, hops):
        return (z + (R - hops if d == 0 else hops)) % R

    def k_send(d, step, h):
        part = KV.at[c, k_block(d, step - 1), pl.ds(h * H, H)]
        return remote(part, part, ks.at[d, step - 1, h], kr.at[d, step - 1, h], p.dev(dz=1 if d == 0 else R - 1))

    def k_arrived(d, step, h):
        part = KV.at[c, k_block(d, step), pl.ds(h * H, H)]
        remote(
            part, part, ks.at[d, step - 1, h], kr.at[d, step - 1, h], p.dev(dz=1 if d == 0 else R - 1)
        ).wait_recv()

    def mirror(b):
        return remote(KV.at[c, b], KV.at[c, b], ms.at[b], mr.at[b], p.sibling())

    def mirrored(b):
        part = KV.at[1 - c, b]
        remote(part, part, ms.at[b], mr.at[b], p.sibling()).wait_recv()

    def k_first():
        own[0].wait()
        own[1].wait()

        @pl.loop(1, R)
        def _(t):
            y_wait(t, 0)
            y_wait(t, 1)

        for h in range(2):
            k_send(0, 1, h).start()
            k_send(1, 1, h).start()
        mirror(z).start()

    def k_step(step):
        for h in range(2):
            k_arrived(0, step - 1, h)
            if step < K or h == 0:
                k_send(0, step, h).start()
            k_arrived(1, step - 1, h)
            if step < K or h == 1:
                k_send(1, step, h).start()
        mirror(k_block(0, step - 1)).start()
        mirror(k_block(1, step - 1)).start()

    def spread(t):
        for d in range(2):
            q_send(d, t).start()

    def forward(t):
        for d in range(2):
            q_arrived(d, t)
            f_send(d, t).start()

    def d_first():
        own[4].wait()

        @pl.loop(1, R)
        def _(t):
            y_wait(t, 4)

        d_send(0, 0).start()
        d_send(1, 0).start()

    def d_second():
        d_arrived(0, 0)
        d_send(0, 1).start()
        d_arrived(1, 0)

    def stats_arrived():
        @pl.loop(1, R)
        def _(t):
            n = (y + t) % R
            remote(LS.at[n], LS.at[n], ls_s.at[0, 0], ls_r.at[n], p.dev(dy=1)).wait_recv()

        pl.when(ls_home)(ls_own.wait)

        @pl.when(jnp.logical_not(ls_home))
        def _():
            remote(LS.at[y], LS.at[y], ls_s.at[0, 0], ls_r.at[y], p.dev(dy=1)).wait_recv()

        lists = LS[:, 2 * GROUP, :]
        shard = jnp.floor(lists / X)
        chip = jnp.floor(shard / 2)
        ky = jnp.floor(chip / R)
        key = ((shard - 2 * chip) * R + chip - R * ky) * R + ky
        LI[...] = jnp.where(lists - X * shard == x.astype(jnp.float32), key, -1.0).astype(jnp.int32)

    key_at = lax.broadcasted_iota(jnp.int32, (KB, QB), 0) + (x % 2) * KB
    causal = key_at <= lax.broadcasted_iota(jnp.int32, (KB, QB), 1)

    def own_terms(t):
        n = (y + p.far(t)) % R
        kv, vv = KV[c, z, n, 0], KV[c, z, n, 1]
        results = [grads(*load_query(QD, DL, LS, n, x // 2, g), kv, vv, causal) for g in range(GROUP)]
        for g in range(GROUP):
            dq0[:, n, :, g * HD : (g + 1) * HD] = results[g][0].reshape(2, KB, HD)
        dkv0[n, 0] = sum(r[1] for r in results)
        dkv0[n, 1] = sum(r[2] for r in results)

    own[2].wait()
    own[3].wait()
    spread(0)
    for t in range(1, R):
        y_wait(t, 2)
        y_wait(t, 3)
        spread(t)
        if t > 1:
            forward(t - 2)
        if t == 1:
            k_first()
        if t == 2:
            d_first()
            stats_arrived()
        if t == 3:
            d_second()
        if t in (3, 5, 7):
            k_step((t + 1) // 2)
        if t >= 4:
            for e in ((0, 1), (2, 3), (4,), (5,))[t - 4]:
                own_terms(e)

    forward(R - 2)
    k_arrived(0, K, 0)
    k_arrived(1, K, 1)
    mirror(k_block(0, K)).start()
    own_terms(R - 2)
    forward(R - 1)
    own_terms(R - 1)
    @pl.loop(0, R)
    def _(t):
        f_arrived(0, t)
        f_arrived(1, t)

    d_arrived(0, 1)

    @pl.loop(0, R)
    def _(b):
        mirrored(b)

    ls_each(lambda copy: copy.wait_send())

    @pl.loop(1, R)
    def _(t):
        for i in range(5):
            y_send(t, i).wait_send()

    @pl.loop(0, R)
    def _(t):
        for d in range(2):
            q_send(d, t).wait_send()
            f_send(d, t).wait_send()
        mirror(t).wait_send()

    d_send(0, 0).wait_send()
    d_send(1, 0).wait_send()
    d_send(0, 1).wait_send()
    for step in range(1, K + 1):
        for h in range(2):
            if step < K or h == 0:
                k_send(0, step, h).wait_send()
            if step < K or h == 1:
                k_send(1, step, h).wait_send()


def gather(R, X, q, do, o, k, v, ls):
    K = R // 2
    rows = q.shape[0]
    anyspace = pl.BlockSpec(memory_space=pl.ANY)
    vmem = pl.BlockSpec(memory_space=pltpu.VMEM)
    dma = pltpu.SemaphoreType.DMA
    f32 = jnp.float32
    return pl.pallas_call(
        functools.partial(gather_kernel, R, X),
        out_shape=(
            jax.ShapeDtypeStruct((X, R, 2, rows, WIDE), jnp.bfloat16),
            jax.ShapeDtypeStruct((2, R, R, 2, rows, HD), jnp.bfloat16),
            jax.ShapeDtypeStruct((X, R, 8, QB), f32),
            jax.ShapeDtypeStruct((R,) + ls.shape[1:], f32),
            jax.ShapeDtypeStruct((R, QB), jnp.int32),
            jax.ShapeDtypeStruct((2, R, rows, WIDE), f32),
            jax.ShapeDtypeStruct((R, 2, rows, HD), f32),
        ),
        in_specs=[anyspace] * 6,
        out_specs=(vmem,) * 7,
        scratch_shapes=[
            pltpu.VMEM((R, 8, QB), f32),
            pltpu.VMEM(do.shape, do.dtype),
            pltpu.VMEM(o.shape, o.dtype),
            dma((5, R)),
            dma((5, R)),
            dma((2, X)),
            dma((R,)),
            dma((8,)),
            dma((2, R)),
            dma((2, R)),
            dma((2, R)),
            dma((2, R)),
            dma((2, 2)),
            dma((2, 2)),
            dma((2, K, 2)),
            dma((2, K, 2)),
            dma((R,)),
            dma((R,)),
        ],
        compiler_params=pltpu.CompilerParams(
            collective_id=1, has_side_effects=True, vmem_limit_bytes=20 << 20
        ),
        name="gather_rings",
    )(*(pltpu.with_memory_space_constraint(a, pltpu.HBM) for a in (q, do, o, k, v)), ls)


def pair_kernel(LI, QD, KV, DL, LS, dq0, dkv0, dq, dkv, pairs):
    X, R = QD.shape[:2]
    x = lax.axis_index("head")
    s = lax.axis_index("seq")
    c, z = s % 2, (s // 2) % R
    own_b = x // 2
    blocks = 2 * R * R
    listed = GROUP * NSEL

    def scan(i, count):
        dq[i // R, i % R] = jnp.zeros(dq.shape[2:], jnp.float32)
        for e in range(blocks // (X * R)):
            dkv[i * (blocks // (X * R)) + e] = jnp.zeros(dkv.shape[1:], jnp.float32)
        for e in range(2 * R * listed // (X * R)):
            k = i * (2 * R * listed // (X * R)) + e
            key = LI[quot(k, 2 * listed), rest(k, 2 * listed)]
            pairs[count] = quot(k, NSEL) * blocks + key
            count += (key >= 0).astype(jnp.int32)
        return count

    count = lax.fori_loop(0, X * R, scan, jnp.int32(0))
    for e in range(UNROLL):
        pairs[count + e] = 0

    @pl.loop(0, R)
    def _(n):
        dq[pl.ds(2 * own_b, 2), n] = dq0[:, n]
        dkv[(c * R + z) * R + n] = dkv0[n]

    @pl.loop(0, (count + UNROLL - 1) // UNROLL)
    def _(t):
        results = []
        for u in range(UNROLL):
            i = t * UNROLL + u
            code = pairs[i]
            unit, key = quot(code, blocks), rest(code, blocks)
            g, b, n = rest(unit, GROUP), rest(quot(unit, GROUP), 2), quot(unit, 2 * GROUP)
            qv, dov, lse, delta = load_query(QD, DL, LS, n, b, g)
            lse = lse + jnp.where(i < count, 0.0, 1e30)
            results.append((n, b, g, key, grads(qv, dov, lse, delta, KV[key, 0], KV[key, 1])))
        for n, b, g, key, out in results:
            dq[pl.ds(2 * b, 2), n, :, columns(g)] += out[0].reshape(2, KB, HD)
            dkv[key, 0] += out[1]
            dkv[key, 1] += out[2]


def pair_grads(LI, QD, KV, DL, LS, dq0, dkv0):
    vmem = pl.BlockSpec(memory_space=pltpu.VMEM)
    smem = pl.BlockSpec(memory_space=pltpu.SMEM)
    X, R = QD.shape[:2]
    flat = KV.reshape((2 * R * R,) + KV.shape[3:])
    dq, dkv = pl.pallas_call(
        pair_kernel,
        out_shape=(
            jax.ShapeDtypeStruct(QD.shape[:2] + QD.shape[3:], jnp.float32),
            jax.ShapeDtypeStruct(flat.shape, jnp.float32),
        ),
        in_specs=[smem] + [vmem] * 6,
        out_specs=(vmem,) * 2,
        scratch_shapes=[pltpu.SMEM((2 * R * GROUP * NSEL + UNROLL,), jnp.int32)],
        compiler_params=pltpu.CompilerParams(vmem_limit_bytes=28 << 20),
        name="pair_grads",
    )(LI, QD, flat, DL, LS, dq0, dkv0)
    return dq, dkv.reshape(KV.shape)


def reduce_kernel(
    R, X, dq, dkv, gq, gk, gv, sf, sp, fq, rq, sm, mk, rk, bq, bk,
    ys, yr, loc, fs, fr, qs, qr, ms, mr, ks, kr,
):
    p = Place(R, X)
    K = R // 2
    H = R // PARTS
    x, y, z, c = p.x, p.y, p.z, p.c
    rows = dq.shape[2]
    half = rows // 2
    p.barrier(False)
    f32 = jnp.float32

    def piece(t):
        return (y + p.far(R - 1 - t)) % R

    def x_to(d):
        return p.dev(dx=1 if d == 0 else X - 1)

    def z_to(d):
        return p.dev(dz=1 if d == 0 else R - 1)

    def part_q(dx, n, at=slice(None)):
        return dq[(x + dx) % X, n, at] * SCALE

    def part_kv(core, b, at=slice(None)):
        part = dkv[core, b, at]
        return jnp.concatenate([part[:, :1] * SCALE, part[:, 1:]], axis=1)

    def f_send(d, t):
        return remote(sf.at[d, t], fq.at[d, t], fs.at[d, t], fr.at[d, t], x_to(d))

    def f_start(t):
        for d in range(2):
            sf[d, t] = part_q(2, piece(t), pl.ds(d * half, half)).astype(jnp.bfloat16)
            f_send(d, t).start()

    def q_send(d, t, late):
        src = (fq if late else sp).at[d, t]
        dst = rq.at[d, t, pl.ds((d if late else 1 - d) * half, half)]
        return remote(src, dst, qs.at[late, d, t], qr.at[late, d, t], x_to(d))

    def q_plain(t):
        for d in range(2):
            at = pl.ds((1 - d) * half, half)
            sp[d, t] = part_q(1 if d == 0 else X - 1, piece(t), at).astype(jnp.bfloat16)
            q_send(d, t, 0).start()

    def q_add(t):
        q_plain(t)
        for d in range(2):
            f_send(d, t).wait_recv()
            mine = part_q(1 if d == 0 else X - 1, piece(t), pl.ds(d * half, half))
            fq[d, t] = (mine + fq[d, t].astype(f32)).astype(jnp.bfloat16)
            q_send(d, t, 1).start()

    def mirror(b):
        return remote(sm.at[b], mk.at[b], ms.at[b], mr.at[b], p.sibling())

    def m_start(b):
        sm[b] = part_kv(1 - c, b).astype(jnp.bfloat16)
        mirror(b).start()

    def owner(d, step):
        far = K + 1 - step
        return (z + (far if d == 0 else R - far)) % R

    def k_send(d, step, h):
        src = mk.at[owner(d, step), pl.ds(h * H, H)]
        return remote(src, rk.at[d, step - 1, h], ks.at[d, step - 1, h], kr.at[d, step - 1, h], z_to(d))

    def k_one(d, step, h):
        b = owner(d, step)
        at = pl.ds(h * H, H)
        total = mk[b, at].astype(f32) + part_kv(c, b, at)
        if step > 2 or (step == 2 and h // (PARTS // 2) == d):
            k_send(d, step - 1, h).wait_recv()
            total = total + rk[d, step - 2, h].astype(f32)
        mk[b, at] = total.astype(jnp.bfloat16)
        k_send(d, step, h).start()

    def k_mirrored(step):
        mirror(owner(0, step)).wait_recv()
        if step > 1:
            mirror(owner(1, step)).wait_recv()

    def k_early(step):
        for i in range(PARTS // 2):
            k_one(0, step, PARTS // 2 + i)
            k_one(1, step, i)

    def k_late(step):
        for i in range(PARTS // 2):
            k_one(0, step, i)
            k_one(1, step, PARTS // 2 + i)

    m_start((z + K) % R)
    pl.loop(0, R)(f_start)
    for far in range(K - 1, 0, -1):
        m_start((z + far) % R)
        m_start((z + R - far) % R)
    m_start(z)

    def out_refs(n, head):
        qcol = pl.ds(pl.multiple_of(head * WIDE, WIDE), WIDE)
        kcol = pl.ds(pl.multiple_of(head * HD, HD), HD)
        return (
            (bq.at[n], gq.at[:, qcol]),
            (bk.at[n, 0], gk.at[:, kcol]),
            (bk.at[n, 1], gv.at[:, kcol]),
        )

    def y_send(t, i):
        src, dst = out_refs(piece(t), y)[i]
        return remote(src, dst, ys.at[i, t], yr.at[i, y], p.dev(dy=p.far(R - 1 - t)))

    def y_wait(t, i):
        n = piece(t)
        src, dst = out_refs(n, n)[i]
        remote(src, dst, ys.at[i, t], yr.at[i, n], p.dev(dy=p.far(R - 1 - t))).wait_recv()

    own = [pltpu.make_async_copy(src, dst, loc.at[i]) for i, (src, dst) in enumerate(out_refs(y, y))]

    def q_total(t):
        for d in range(2):
            q_send(d, t, 0).wait_recv()
            q_send(d, t, 1).wait_recv()
        n = piece(t)
        bq[n] = (part_q(0, n) + rq[0, t].astype(f32) + rq[1, t].astype(f32)).astype(jnp.bfloat16)

    def q_home(t):
        q_total(t)
        y_send(t, 0).start()

    def k_out(n, i):
        return remote(out_refs(n, y)[i][0], out_refs(n, y)[i][1], ys.at[i, n], yr.at[i, y], p.at(x, n, z))

    def k_home(h):
        at = pl.ds(h * H, H)
        total = part_kv(c, z, at) + mk[z, at].astype(f32)
        for d in range(2):
            k_send(d, K, h).wait_recv()
            total = total + rk[d, K - 1, h].astype(f32)
        bk[at] = total.astype(jnp.bfloat16)

        @pl.loop(h * H, (h + 1) * H)
        def _(n):
            @pl.when(n != y)
            def _():
                k_out(n, 1).start()
                k_out(n, 2).start()

            @pl.when(n == y)
            def _():
                own[1].start()
                own[2].start()

    k_mirrored(1)
    k_late(1)
    k_mirrored(2)
    k_early(2)
    pl.loop(0, 4)(q_add)
    k_late(2)
    pl.loop(4, R)(q_add)
    k_mirrored(3)
    k_early(3)
    pl.loop(0, 2)(q_home)
    k_late(3)
    pl.loop(2, 4)(q_home)
    k_mirrored(4)
    k_early(4)
    pl.loop(4, 6)(q_home)
    k_late(4)
    pl.loop(6, R - 1)(q_home)
    q_total(R - 1)
    own[0].start()
    mirror(z).wait_recv()
    for i in range(PARTS // 2):
        k_home(i)
        k_home(PARTS // 2 + i)

    @pl.loop(0, R - 1)
    def _(t):
        for i in range(3):
            y_wait(t, i)

    for copy in own:
        copy.wait()

    @pl.loop(0, R - 1)
    def _(t):
        y_send(t, 0).wait_send()

    @pl.loop(0, R)
    def _(n):
        @pl.when(n != y)
        def _():
            k_out(n, 1).wait_send()
            k_out(n, 2).wait_send()

    @pl.loop(0, R)
    def _(t):
        for d in range(2):
            f_send(d, t).wait_send()
            q_send(d, t, 0).wait_send()
            q_send(d, t, 1).wait_send()
        mirror(t).wait_send()

    for step in range(1, K + 1):
        for h in range(PARTS):
            for d in range(2):
                if step > 1 or h // (PARTS // 2) == d:
                    k_send(d, step, h).wait_send()


def reduce(R, X, dq, dkv):
    K = R // 2
    rows = dq.shape[2]
    anyspace = pl.BlockSpec(memory_space=pl.ANY)
    vmem = pl.BlockSpec(memory_space=pltpu.VMEM)
    dma = pltpu.SemaphoreType.DMA
    bf16 = jnp.bfloat16
    return pl.pallas_call(
        functools.partial(reduce_kernel, R, X),
        out_shape=(
            jax.ShapeDtypeStruct((rows, R * WIDE), bf16),
            jax.ShapeDtypeStruct((rows, R * HD), bf16),
            jax.ShapeDtypeStruct((rows, R * HD), bf16),
        ),
        in_specs=[vmem] * 2,
        out_specs=(anyspace,) * 3,
        scratch_shapes=[
            pltpu.VMEM((2, R, rows // 2, WIDE), bf16),
            pltpu.VMEM((2, R, rows // 2, WIDE), bf16),
            pltpu.VMEM((2, R, rows // 2, WIDE), bf16),
            pltpu.VMEM((2, R, rows, WIDE), bf16),
            pltpu.VMEM(dkv.shape[1:], bf16),
            pltpu.VMEM(dkv.shape[1:], bf16),
            pltpu.VMEM((2, K, PARTS, R // PARTS) + dkv.shape[3:], bf16),
            pltpu.VMEM(dq.shape[1:], bf16),
            pltpu.VMEM(dkv.shape[2:], bf16),
            dma((3, R)),
            dma((3, R)),
            dma((3,)),
            dma((2, R)),
            dma((2, R)),
            dma((2, 2, R)),
            dma((2, 2, R)),
            dma((R,)),
            dma((R,)),
            dma((2, K, PARTS)),
            dma((2, K, PARTS)),
        ],
        compiler_params=pltpu.CompilerParams(
            collective_id=2, has_side_effects=True, vmem_limit_bytes=26 << 20
        ),
        name="reduce_rings",
    )(dq, dkv)


def finish_kernel(*refs):
    n = len(refs) // 2
    sems = refs[-1]
    copies = [pltpu.make_async_copy(refs[i], refs[n + i], sems.at[i]) for i in range(n)]
    for copy in copies:
        copy.start()
    for copy in copies:
        copy.wait()


def finish(*arrays):
    anyspace = pl.BlockSpec(memory_space=pl.ANY)
    return pl.pallas_call(
        finish_kernel,
        out_shape=tuple(jax.ShapeDtypeStruct(a.shape, a.dtype) for a in arrays),
        in_specs=[anyspace] * len(arrays),
        out_specs=(pl.BlockSpec(memory_space=pltpu.HBM),) * len(arrays),
        scratch_shapes=[pltpu.SemaphoreType.DMA((len(arrays),))],
        name="finish",
    )(*arrays)


def body(R, X, queries, keys, values, outputs_saved, grad_out, lse, block_lists):
    heads = lse.T
    stats = jnp.stack(
        [
            jnp.concatenate(
                [heads[i * GROUP : (i + 1) * GROUP, b * QB : (b + 1) * QB] for b in range(2)], axis=0
            )
            for i in range(2)
        ]
    )
    lists = lax.dynamic_slice_in_dim(block_lists, 2 * lax.axis_index("seq"), 2, 0)
    lists = lists.reshape(2, 2, GROUP, NSEL).transpose(1, 0, 2, 3).reshape(2, 1, 2 * GROUP * NSEL)
    lists = jnp.pad(lists.astype(jnp.float32), ((0, 0), (0, 7), (0, QB - 2 * GROUP * NSEL)))
    stats = jnp.concatenate([stats, lists], axis=1)
    QD, KV, DL, LS, LI, dq0, dkv0 = gather(
        R, X, queries, grad_out, outputs_saved, keys, values, stats
    )
    dq, dkv = pair_grads(LI, QD, KV, DL, LS, dq0, dkv0)
    parts = reduce(R, X, dq, dkv)
    return finish(*(pltpu.with_memory_space_constraint(a, pltpu.VMEM) for a in parts))


def solution(mesh):
    R = math.isqrt(mesh.shape["seq"] // 2)
    X = mesh.shape["head"]
    in_specs = (
        P(("seq", "head"), None),
        P(("seq", "head"), None),
        P(("seq", "head"), None),
        P(("seq", "head"), None),
        P(("seq", "head"), None),
        P("seq", "head"),
        P(None, "head", None),
    )
    out_specs = (P(("seq", "head"), None), P(("seq", "head"), None), P(("seq", "head"), None))
    return jax.shard_map(
        functools.partial(body, R, X), mesh=mesh, in_specs=in_specs, out_specs=out_specs, check_vma=False
    )
```
